256 devices in a mesh: aux: 4 (over y), shell: 64 (over z, x, core).
Axes of the slice: x: 4, y: 4, z: 8, core: 2. Of those that a mesh axis runs over, the one named last changes fastest.
Arguments:
- three_center: bfloat16 [64, 40, 4, 128, 128], P('shell', None, 'aux'), may hold values from -6 to 6
- occupied: bfloat16 [8192, 384], P('shell'), may hold values from -0.01953125 to 0.01953125
- tile_blocks: int32 [4, 64, 40], P('aux', 'shell'), may hold values from 0 to 63, as said below
Outputs:
- exchange_matrix: float32 [8192, 8192], P('shell', 'aux')
The draws below stay inside these ranges and needn't reach their ends.
Inputs may be any that keep to these rules, and one draw needn't show every extreme that they name: In each row tile_blocks[a, g] the 40 mu blocks are distinct, and the first is g itself.
All inputs are finite; a program needn't handle non-finite values.
Results may differ from the reference program's by a relative error of at most 0.014.
Values may be sent and summed in bfloat16 or wider, within the bound.
A program may use at most 64 MiB of HBM per device.

```python
import jax
import jax.numpy as jnp
from jax import lax

BLK = 128
BASIS_BLOCKS = 64
NBAS = 8192
OCC = 384
AUX_DEV = 1
SLAB = 4
AUX_BLOCKS = 4
TILE_BLK = 40


def draw_tile_blocks(key, part):
    key = jax.random.fold_in(key, 11)
    favour_key, jitter_key = jax.random.split(key)
    preference_weight = jax.random.randint(favour_key, (AUX_BLOCKS, 1, BASIS_BLOCKS), 0, 4) * 700
    random_perturbation = jax.random.randint(jitter_key, (AUX_BLOCKS, BASIS_BLOCKS, BASIS_BLOCKS), 0, 1000)
    row_positions = lax.broadcasted_iota(jnp.int32, (AUX_BLOCKS, BASIS_BLOCKS, BASIS_BLOCKS), 1)
    column_positions = lax.broadcasted_iota(jnp.int32, (AUX_BLOCKS, BASIS_BLOCKS, BASIS_BLOCKS), 2)
    diagonal_boost = jnp.where(row_positions == column_positions, 100000, 0)
    block_ordering = (preference_weight + random_perturbation + diagonal_boost) * BASIS_BLOCKS + column_positions
    _, chosen = lax.top_k(block_ordering, TILE_BLK)
    return chosen.astype(jnp.int32)


def block_levels(key, shape, cuts, low, high):
    factor_of = 1.0
    for dim, shards_of in cuts:
        steps = jax.random.uniform(jax.random.fold_in(jax.random.fold_in(key, 6), dim), (shards_of,), jnp.float32, low / len(cuts), high / len(cuts))
        factor_of = factor_of * jnp.repeat(jnp.exp(steps), shape[dim] // shards_of).reshape((-1,) + (1,) * (len(shape) - 1 - dim))
    return factor_of


def gaussian(rng, dims, spread, most, shards=(), held_as=jnp.bfloat16):
    gain = block_levels(rng, dims, shards, -0.22, 0.18) if shards else 1.0
    values = jax.random.normal(rng, dims, jnp.float32) * spread * gain
    return jnp.minimum(jnp.maximum(values, -most), most).astype(held_as)


def setup_inputs(seed: int = 0) -> dict:
    splits = jax.random.split(jax.random.key(seed), 4)
    return {
        "three_center": gaussian(splits[0], (BASIS_BLOCKS, TILE_BLK, SLAB, BLK, BLK), 1.0, 6.0, ((0, 64), (2, 4))),
        "occupied": gaussian(splits[1], (NBAS, OCC), (0.55 / ((SLAB * OCC) ** 0.25 * (TILE_BLK * BLK) ** 0.5)), 0.01953125, ((0, 64),)),
        "tile_blocks": draw_tile_blocks(jax.random.fold_in(splits[3], 71), 0),
    }


def reference(three_center, occupied, tile_blocks):
    initial = jnp.zeros((BASIS_BLOCKS, SLAB, BLK, OCC), jnp.float32)

    def add_block(running, lam_block):
        block_tiles = lax.dynamic_index_in_dim(three_center, lam_block, 0, keepdims=False).astype(jnp.float32)
        orbital_rows = lax.dynamic_slice_in_dim(occupied, lam_block * BLK, BLK, 0).astype(jnp.float32)
        halfway = jnp.einsum('tpxl,li->tpxi', block_tiles, orbital_rows).astype(jnp.bfloat16)
        halfway = lax.optimization_barrier(halfway).astype(jnp.float32)
        for aux_block in range(AUX_BLOCKS):
            targets = lax.dynamic_index_in_dim(tile_blocks[aux_block], lam_block, 0, keepdims=False).astype(jnp.int32)
            running = running.at[targets, aux_block * AUX_DEV:(aux_block + 1) * AUX_DEV].add(
                halfway[:, aux_block * AUX_DEV:(aux_block + 1) * AUX_DEV])
        return running, None

    running, _ = lax.scan(add_block, initial, jnp.arange(BASIS_BLOCKS).astype(jnp.int32))
    fitted = running.astype(jnp.bfloat16)
    fitted_rows = jnp.transpose(fitted, (0, 2, 1, 3)).reshape(NBAS, SLAB * OCC)
    return jnp.dot(fitted_rows, fitted_rows.T, preferred_element_type=jnp.float32)
```

```python
import jax
import jax.numpy as jnp
from jax import lax
from jax.experimental import pallas as pl
from jax.experimental.pallas import tpu as pltpu
from jax.sharding import PartitionSpec as P

MESH = pl.DeviceIdType.MESH
BLK = 128
OCC = 384
TILES = 40
NY, NZ, NX = 4, 8, 4

WINDOW = [(dz, dx, e) for dz in range(2) for dx in range(2) for e in range(2)]
PARTS = [(2 * k, 2 * j) for k in range(4) for j in range(2)]
ROWS = [(dx, e) for dx in range(NX) for e in range(2)]


def greeted():
    out = set()
    for dz, dx, e in WINDOW:
        out.add((0, dz, dx, e))
        out.add((0, -dz % NZ, -dx % NX, e))
    for dz, dx in PARTS:
        out.add((0, dz, dx, 0))
    for dz in range(NZ):
        out.add((0, dz, 0, 0))
    for dy in range(NY):
        for dx, e in ROWS:
            out.add((dy, 0, dx, e))
    out.discard((0, 0, 0, 0))
    return sorted(out)


def kernel(
    slots_ref, tiles_ref, occ_ref, out_ref,
    dense, tiles_in, occ_in, part, part_in, rows, cols, pair, pair_in,
    s_tile, r_tile, s_occ, r_occ, s_part, r_part, s_row, r_row, s_col, r_col, s_pair, r_pair,
):
    y = lax.axis_index("aux")
    shell = lax.axis_index("shell")
    z, x, c = shell // (2 * NX), (shell // 2) % NX, shell % 2

    def device(dy, zz, xx, cc):
        return ((y + dy) % NY, zz * (2 * NX) + xx * 2 + cc)

    def near(dy=0, dz=0, dx=0, e=0):
        return device(dy, (z + dz) % NZ, (x + dx) % NX, (c + e) % 2)

    def copy(src, dst, send, recv, to):
        return pltpu.make_async_remote_copy(
            src_ref=src, dst_ref=dst, send_sem=send, recv_sem=recv, device_id=to, device_id_type=MESH
        )

    peers = greeted()
    barrier = pltpu.get_barrier_semaphore()
    for dy, dz, dx, e in peers:
        pl.semaphore_signal(barrier, inc=1, device_id=near(dy, dz, dx, e), device_id_type=MESH)

    def target(dz, dx, e):
        tc = (c + e) % 2
        sign = 1 - 2 * tc
        return (z - sign * dz + NZ) % NZ, (x - sign * dx + NX) % NX, tc

    for s, (dz, dx, e) in enumerate(WINDOW):
        tz, tx, tc = target(dz, dx, e)
        to = tiles_in.at[0] if s == 0 else dense.at[s]

        def fill(i, carry, to=to, tz=tz, tx=tx, tc=tc):
            k, j = i // 2, i % 2
            block = ((tz + 2 * k) % NZ) * (2 * NX) + ((tx + 2 * j) % NX) * 2 + tc
            slot = slots_ref[block]
            held = tiles_ref[jnp.maximum(slot - 1, 0)]
            to[i] = jnp.where(slot > 0, held, jnp.zeros_like(held))
            return carry

        lax.fori_loop(0, 8, fill, 0)
    occ_in[0] = occ_ref[...]

    pl.semaphore_wait(barrier, len(peers))

    sends = []
    for s, w in enumerate(WINDOW):
        if s:
            tz, tx, tc = target(*w)
            cp = copy(occ_ref, occ_in.at[s], s_occ.at[s], r_occ.at[s], device(0, tz, tx, tc))
            cp.start()
            sends.append(cp)
    first = []
    for s, w in enumerate(WINDOW):
        if s:
            tz, tx, tc = target(*w)
            cp = copy(dense.at[s], tiles_in.at[s], s_tile.at[s], r_tile.at[s], device(0, tz, tx, tc))
            cp.start()
            first.append(cp)
    for cp in sends + first:
        cp.wait_recv()

    def work(i, carry):
        lhs = jnp.concatenate([tiles_in[s, i] for s in range(8)], axis=1)
        rhs = occ_in[...].reshape(8 * BLK, OCC)
        part[i] = jnp.dot(lhs, rhs, preferred_element_type=jnp.float32).astype(jnp.bfloat16)
        return carry

    lax.fori_loop(0, 8, work, 0)
    second = []
    for i, (dz, dx) in enumerate(PARTS):
        if i:
            cp = copy(part.at[i], part_in.at[i], s_part.at[i], r_part.at[i], near(0, dz, dx, 0))
            cp.start()
            second.append(cp)
    total = part[0].astype(jnp.float32)
    for i, cp in enumerate(second):
        cp.wait_recv()
        total = total + part_in[i + 1].astype(jnp.float32)
    rows[0] = total.astype(jnp.bfloat16)
    cols[z] = total.astype(jnp.bfloat16)

    third = []
    for dz in range(1, NZ):
        cp = copy(rows.at[0], cols.at[z], s_col.at[dz], r_col.at[dz], near(0, dz, 0, 0))
        cp.start()
        third.append(cp)
    across = []
    for r, (dx, e) in enumerate(ROWS):
        if r:
            cp = copy(rows.at[0], rows.at[r], s_row.at[r], r_row.at[r], near(0, 0, -dx, e))
            cp.start()
            across.append(cp)
    for cp in across:
        cp.wait_recv()
    for dz in range(1, NZ):
        copy(rows.at[0], cols.at[(z - dz + NZ) % NZ], s_col.at[dz], r_col.at[dz], near(0, dz, 0, 0)).wait_recv()

    fourth = []
    for dy in (2, 1, 3, 0):
        ty = (y + dy) % NY
        rhs = cols[pl.ds(2 * ty, 2)].reshape(2 * BLK, OCC)

        def product(r, carry, dy=dy, rhs=rhs):
            both = lax.dot_general(
                rows[r], rhs, (((1,), (1,)), ((), ())), preferred_element_type=jnp.float32
            )
            pair[dy * 8 + r] = both.astype(jnp.bfloat16)
            return carry

        lax.fori_loop(0, 8, product, 0)
        for r, (dx, e) in enumerate(ROWS):
            if dy or r:
                i = dy * 8 + r
                cp = copy(pair.at[i], pair_in.at[i], s_pair.at[i], r_pair.at[i], near(dy, 0, dx, e))
                cp.start()
                fourth.append(cp)
    for cp in fourth:
        cp.wait_recv()
    for r, (dx, e) in enumerate(ROWS):
        own = pair[0] if r == 0 else pair_in[r]
        value = own.astype(jnp.float32)
        for dy in range(1, NY):
            value = value + pair_in[dy * 8 + r].astype(jnp.float32)
        at = ((x - dx + NX) % NX) * 2 + (c + e) % 2
        for zz in range(2):
            lane = pl.multiple_of(zz * (8 * BLK) + at * BLK, BLK)
            out_ref[:, pl.ds(lane, BLK)] = value[:, zz * BLK:(zz + 1) * BLK]
    for cp in sends + first + second + third + across + fourth:
        cp.wait_send()


def body(three_center, occupied, tile_blocks):
    tiles = three_center.reshape(TILES, BLK, BLK)
    targets = tile_blocks.reshape(TILES)
    hit = targets[None, :] == jnp.arange(NZ * NX * 2, dtype=jnp.int32)[:, None]
    slots = jnp.sum(jnp.where(hit, jnp.arange(1, TILES + 1, dtype=jnp.int32)[None, :], 0), axis=1)
    vmem = pl.BlockSpec(memory_space=pltpu.VMEM)
    bf16 = jnp.bfloat16
    dma = pltpu.SemaphoreType.DMA
    return pl.pallas_call(
        kernel,
        out_shape=jax.ShapeDtypeStruct((BLK, 2048), jnp.float32),
        in_specs=[pl.BlockSpec(memory_space=pltpu.SMEM), vmem, vmem],
        out_specs=vmem,
        scratch_shapes=[
            pltpu.VMEM((8, 8, BLK, BLK), bf16),
            pltpu.VMEM((8, 8, BLK, BLK), bf16),
            pltpu.VMEM((8, BLK, OCC), bf16),
            pltpu.VMEM((8, BLK, OCC), bf16),
            pltpu.VMEM((8, BLK, OCC), bf16),
            pltpu.VMEM((8, BLK, OCC), bf16),
            pltpu.VMEM((8, BLK, OCC), bf16),
            pltpu.VMEM((32, BLK, 2 * BLK), bf16),
            pltpu.VMEM((32, BLK, 2 * BLK), bf16),
            dma((8,)), dma((8,)), dma((8,)), dma((8,)), dma((8,)), dma((8,)),
            dma((8,)), dma((8,)), dma((8,)), dma((8,)), dma((32,)), dma((32,)),
        ],
        compiler_params=pltpu.CompilerParams(
            collective_id=0, has_side_effects=True, vmem_limit_bytes=48 * 1024 * 1024
        ),
        cost_estimate=pl.CostEstimate(flops=1_700_000_000, bytes_accessed=3_000_000, transcendentals=0),
    )(slots, tiles, occupied)


def solution(mesh):
    return jax.shard_map(
        body,
        mesh=mesh,
        in_specs=(P("shell", None, "aux", None, None), P("shell", None), P("aux", "shell", None)),
        out_specs=P("shell", "aux"),
        check_vma=False,
    )
```

```python
import jax
import jax.numpy as jnp
from jax import lax
from jax.experimental import pallas as pl
from jax.experimental.pallas import tpu as pltpu
from jax.sharding import PartitionSpec as P

MESH = pl.DeviceIdType.MESH
BLK = 128
HALF = BLK // 2
OCC = 384
TILES = 40
NY, NZ, NX = 4, 8, 4

WINDOW = [(dz, dx, e) for dz in range(2) for dx in range(2) for e in range(2)]
ROWS = [(dx, e) for dx in range(NX) for e in range(2)]
ORDER = (2, 1, 3, 0)


def greeted():
    out = {(0, 0, 2, 0)}
    for dz, dx, e in WINDOW:
        out.add((0, dz, dx, e))
        out.add((0, -dz % NZ, -dx % NX, e))
    for dz in range(NZ):
        out.add((0, dz, 0, 0))
    for dy in range(NY):
        for dx, e in ROWS:
            out.add((dy, 0, dx, e))
    out.discard((0, 0, 0, 0))
    return sorted(out)


def kernel(
    slots_ref, tiles_hbm, occ_ref, out_ref,
    tiles_ref, dense, tiles_in, occ_in, own, part, part_in, mid, mid_in, rows, cols, pair, pair_in,
    s_load, s_tile, r_tile, s_occ, r_occ, s_part, r_part, s_mid, r_mid, s_row, r_row, s_col, r_col, s_pair, r_pair,
):
    y = lax.axis_index("aux")
    shell = lax.axis_index("shell")
    z, x, c = shell // (2 * NX), (shell // 2) % NX, shell % 2

    def device(dy, zz, xx, cc):
        return ((y + dy) % NY, zz * (2 * NX) + xx * 2 + cc)

    def near(dy=0, dz=0, dx=0, e=0):
        return device(dy, (z + dz) % NZ, (x + dx) % NX, (c + e) % 2)

    def copy(src, dst, send, recv, to):
        return pltpu.make_async_remote_copy(
            src_ref=src, dst_ref=dst, send_sem=send, recv_sem=recv, device_id=to, device_id_type=MESH
        )

    started = []
    load = pltpu.make_async_copy(tiles_hbm, tiles_ref, s_load)
    load.start()
    peers = greeted()
    barrier = pltpu.get_barrier_semaphore()
    for dy, dz, dx, e in peers:
        pl.semaphore_signal(barrier, inc=1, device_id=near(dy, dz, dx, e), device_id_type=MESH)

    def target(dz, dx, e):
        tc = (c + e) % 2
        sign = 1 - 2 * tc
        return (z - sign * dz + NZ) % NZ, (x - sign * dx + NX) % NX, tc

    def spread(k):
        def fill(i, carry):
            s, j = i // 2, i % 2
            tz, tx, tc = target(s // 4, (s // 2) % 2, s % 2)
            block = ((tz + 2 * k) % NZ) * (2 * NX) + ((tx + 2 * j) % NX) * 2 + tc
            slot = slots_ref[block]
            held = tiles_ref[jnp.maximum(slot - 1, 0)]
            dense[k, s, j] = jnp.where(slot > 0, held, jnp.zeros_like(held))
            return carry

        lax.fori_loop(0, 16, fill, 0)

    occ_in[0] = occ_ref[...]
    load.wait()
    spread(ORDER[0])
    pl.semaphore_wait(barrier, len(peers))
    for s, w in enumerate(WINDOW):
        if s:
            cp = copy(occ_ref, occ_in.at[s], s_occ.at[s], r_occ.at[s], device(0, *target(*w)))
            cp.start()
            started.append(cp)
    orbital = list(started)
    arriving = {}
    for k in ORDER:
        if k != ORDER[0]:
            spread(k)
        arriving[k] = []
        for s, w in enumerate(WINDOW):
            if s:
                cp = copy(dense.at[k, s], tiles_in.at[k, s], s_tile.at[k, s], r_tile.at[k, s], device(0, *target(*w)))
                cp.start()
                arriving[k].append(cp)
        started += arriving[k]
    for cp in orbital:
        cp.wait_recv()

    facing = {}
    for k in ORDER:
        for cp in arriving[k]:
            cp.wait_recv()
        lhs = jnp.concatenate(
            [
                jnp.concatenate([dense[k, 0, j]] + [tiles_in[k, s, j] for s in range(1, 8)], axis=1)
                for j in range(2)
            ],
            axis=0,
        )
        both = jnp.dot(lhs, occ_in[...].reshape(8 * BLK, OCC), preferred_element_type=jnp.float32)
        own[k] = both[:BLK]
        part[k] = both[BLK:].astype(jnp.bfloat16)
        cp = copy(part.at[k], part_in.at[k], s_part.at[k], r_part.at[k], near(0, 0, 2, 0))
        cp.start()
        started.append(cp)
        facing[k] = cp
    along = []
    for k in ORDER:
        facing[k].wait_recv()
        own[k] += part_in[k].astype(jnp.float32)
        if k:
            mid[k] = own[k].astype(jnp.bfloat16)
            cp = copy(mid.at[k], mid_in.at[k], s_mid.at[k], r_mid.at[k], near(0, 2 * k, 0, 0))
            cp.start()
            started.append(cp)
            along.append((k, cp))
    total = own[0]
    for k, cp in along:
        cp.wait_recv()
        total = total + mid_in[k].astype(jnp.float32)
    fitted = total.astype(jnp.bfloat16)
    rows[0] = fitted
    cols[0, z] = fitted[:HALF]
    cols[1, z] = fitted[HALF:]

    across = []
    for r, (dx, e) in enumerate(ROWS):
        if r:
            cp = copy(rows.at[0], rows.at[r], s_row.at[r], r_row.at[r], near(0, 0, -dx, e))
            cp.start()
            across.append(cp)
    started += across
    for h in range(2):
        for dz in (4, 3, 5, 2, 6, 1, 7):
            half = rows.at[0, pl.ds(h * HALF, HALF)]
            cp = copy(half, cols.at[h, z], s_col.at[h, dz], r_col.at[h, dz], near(0, dz, 0, 0))
            cp.start()
            started.append(cp)
    for cp in across:
        cp.wait_recv()

    last = []
    for h in range(2):
        for dz in range(1, NZ):
            there = cols.at[h, (z - dz + NZ) % NZ]
            copy(there, there, s_col.at[h, dz], r_col.at[h, dz], near(0, dz, 0, 0)).wait_recv()
        rhs = cols[h].reshape(NZ * HALF, OCC)
        for r, (dx, e) in enumerate(ROWS):
            block = lax.dot_general(
                rows[r], rhs, (((1,), (1,)), ((), ())), preferred_element_type=jnp.float32
            ).astype(jnp.bfloat16)
            for a in range(NY):
                pair[h, a, r] = block[:, a * BLK:(a + 1) * BLK]
            for dy in (2, 1, 3, 0):
                if dy or r:
                    cp = copy(
                        pair.at[h, (y + dy) % NY, r], pair_in.at[h, dy, r],
                        s_pair.at[h, dy, r], r_pair.at[h, dy, r], near(dy, 0, dx, e),
                    )
                    cp.start()
                    last.append(cp)
    started += last
    for cp in last:
        cp.wait_recv()
    for r, (dx, e) in enumerate(ROWS):
        halves = []
        for h in range(2):
            value = (pair[h, y, 0] if r == 0 else pair_in[h, 0, r]).astype(jnp.float32)
            for dy in range(1, NY):
                value = value + pair_in[h, dy, r].astype(jnp.float32)
            halves.append(value)
        at = ((x - dx + NX) % NX) * 2 + (c + e) % 2
        for zz in range(2):
            lane = pl.multiple_of(zz * (8 * BLK) + at * BLK, BLK)
            out_ref[:, pl.ds(lane, BLK)] = jnp.concatenate(
                [v[:, zz * HALF:(zz + 1) * HALF] for v in halves], axis=1
            )
    for cp in started:
        cp.wait_send()


def body(three_center, occupied, tile_blocks):
    tiles = three_center.reshape(TILES, BLK, BLK)
    targets = tile_blocks.reshape(TILES)
    hit = targets[None, :] == jnp.arange(NZ * NX * 2, dtype=jnp.int32)[:, None]
    slots = jnp.sum(jnp.where(hit, jnp.arange(1, TILES + 1, dtype=jnp.int32)[None, :], 0), axis=1)
    vmem = pl.BlockSpec(memory_space=pltpu.VMEM)
    bf16, f32 = jnp.bfloat16, jnp.float32
    dma = pltpu.SemaphoreType.DMA
    return pl.pallas_call(
        kernel,
        out_shape=jax.ShapeDtypeStruct((BLK, 2048), f32),
        in_specs=[pl.BlockSpec(memory_space=pltpu.SMEM), pl.BlockSpec(memory_space=pl.ANY), vmem],
        out_specs=vmem,
        scratch_shapes=[
            pltpu.VMEM((TILES, BLK, BLK), bf16),
            pltpu.VMEM((4, 8, 2, BLK, BLK), bf16),
            pltpu.VMEM((4, 8, 2, BLK, BLK), bf16),
            pltpu.VMEM((8, BLK, OCC), bf16),
            pltpu.VMEM((4, BLK, OCC), f32),
            pltpu.VMEM((4, BLK, OCC), bf16),
            pltpu.VMEM((4, BLK, OCC), bf16),
            pltpu.VMEM((4, BLK, OCC), bf16),
            pltpu.VMEM((4, BLK, OCC), bf16),
            pltpu.VMEM((8, BLK, OCC), bf16),
            pltpu.VMEM((2, NZ, HALF, OCC), bf16),
            pltpu.VMEM((2, NY, 8, BLK, BLK), bf16),
            pltpu.VMEM((2, NY, 8, BLK, BLK), bf16),
            dma(()),
            dma((4, 8)), dma((4, 8)), dma((8,)), dma((8,)), dma((4,)), dma((4,)), dma((4,)), dma((4,)),
            dma((8,)), dma((8,)), dma((2, 8)), dma((2, 8)), dma((2, NY, 8)), dma((2, NY, 8)),
        ],
        compiler_params=pltpu.CompilerParams(
            collective_id=0, has_side_effects=True, vmem_limit_bytes=60 * 1024 * 1024
        ),
        cost_estimate=pl.CostEstimate(flops=1_700_000_000, bytes_accessed=3_000_000, transcendentals=0),
    )(slots, tiles, occupied)


def solution(mesh):
    return jax.shard_map(
        body,
        mesh=mesh,
        in_specs=(P("shell", None, "aux", None, None), P("shell", None), P("aux", "shell", None)),
        out_specs=P("shell", "aux"),
        check_vma=False,
    )
```

```python
import jax
import jax.numpy as jnp
from jax import lax
from jax.experimental import pallas as pl
from jax.experimental.pallas import tpu as pltpu
from jax.sharding import PartitionSpec as P

MESH = pl.DeviceIdType.MESH
BLK = 128
OCC = 384
TILES = 40
NY, NZ, NX = 4, 8, 4

WINDOW = [(dz, dx, e) for dz in range(2) for dx in range(2) for e in range(2)]
ROWS = [(dx, e) for dx in range(NX) for e in range(2)]
ORDER = (2, 1, 3, 0)
CHUNKS = (0, 1, 3, 2)


def greeted():
    out = set()
    for dz, dx, e in WINDOW:
        out.add((0, dz, dx, e))
        out.add((0, -dz % NZ, -dx % NX, e))
    for dz in range(NZ):
        out.add((0, dz, 0, 0))
    for dy in range(NY):
        out.add((dy, 0, 0, 0))
    for dx, e in ROWS:
        out.add((0, 0, dx, e))
    out.discard((0, 0, 0, 0))
    return sorted(out)


def kernel(
    slots_ref, tiles_hbm, occ_hbm, out_ref,
    tiles_ref, dense, tiles_in, occ_in, own, part, part_in, mid, mid_in, rows, cols, pair, pair_in, done, done_in,
    mirror_in, twin_in, twin, twin_done, twin_mirror,
    s_load, s_load_occ, s_tile, r_tile, s_occ, r_occ, s_part, r_part, s_mid, r_mid, s_row, r_row, s_col, r_col, s_pair, r_pair,
    s_done, r_done, s_mirror, r_mirror, s_twin, r_twin, s_out, r_out, s_back, r_back,
):
    y = lax.axis_index("aux")
    shell = lax.axis_index("shell")
    z, x, c = shell // (2 * NX), (shell // 2) % NX, shell % 2

    def device(dy, zz, xx, cc):
        return ((y + dy) % NY, zz * (2 * NX) + xx * 2 + cc)

    def near(dy=0, dz=0, dx=0, e=0):
        return device(dy, (z + dz) % NZ, (x + dx) % NX, (c + e) % 2)

    def copy(src, dst, send, recv, to):
        return pltpu.make_async_remote_copy(
            src_ref=src, dst_ref=dst, send_sem=send, recv_sem=recv, device_id=to, device_id_type=MESH
        )

    started = []
    load = pltpu.make_async_copy(tiles_hbm, tiles_ref, s_load)
    load.start()
    load_occ = pltpu.make_async_copy(occ_hbm, occ_in.at[0], s_load_occ)
    load_occ.start()
    peers = greeted()
    barrier = pltpu.get_barrier_semaphore()
    for dy, dz, dx, e in peers:
        pl.semaphore_signal(barrier, inc=1, device_id=near(dy, dz, dx, e), device_id_type=MESH)
    zp, zs = z // 2, z % 2
    home = y == zp
    chosen = jnp.where(home, z, 2 * y + jnp.where(y > zp, zs, 1 - zs))
    other = jnp.where(home, z + 1 - 2 * zs, 2 * y + jnp.where(y > zp, 1 - zs, zs))
    shell_of = lambda zz: zz * (2 * NX) + x * 2 + c
    pl.semaphore_signal(barrier, inc=1, device_id=(zp, shell_of(other)), device_id_type=MESH)

    def target(dz, dx, e):
        tc = (c + e) % 2
        sign = 1 - 2 * tc
        return (z - sign * dz + NZ) % NZ, (x - sign * dx + NX) % NX, tc

    def spread(k):
        def fill(i, carry):
            s, j = i // 2, i % 2
            tz, tx, tc = target(s // 4, (s // 2) % 2, s % 2)
            block = ((tz + 2 * k) % NZ) * (2 * NX) + ((tx + 2 * j) % NX) * 2 + tc
            slot = slots_ref[block]
            held = tiles_ref[jnp.maximum(slot - 1, 0)]
            dense[k, s, j] = jnp.where(slot > 0, held, jnp.zeros_like(held))
            return carry

        lax.fori_loop(0, 16, fill, 0)

    load_occ.wait()
    pl.semaphore_wait(barrier, len(peers) + 1)
    for s, w in enumerate(WINDOW):
        if s:
            cp = copy(occ_in.at[0], occ_in.at[s], s_occ.at[s], r_occ.at[s], device(0, *target(*w)))
            cp.start()
            started.append(cp)
    orbital = list(started)
    arriving = {}
    load.wait()
    for k in ORDER:
        spread(k)
        arriving[k] = []
        for s, w in enumerate(WINDOW):
            if s:
                cp = copy(dense.at[k, s], tiles_in.at[k, s], s_tile.at[k, s], r_tile.at[k, s], device(0, *target(*w)))
                cp.start()
                arriving[k].append(cp)
        started += arriving[k]
    for cp in orbital:
        cp.wait_recv()

    facing = {}
    for k in ORDER:
        for cp in arriving[k]:
            cp.wait_recv()
        lhs = jnp.concatenate(
            [
                jnp.concatenate([dense[k, 0, j]] + [tiles_in[k, s, j] for s in range(1, 8)], axis=1)
                for j in range(2)
            ],
            axis=0,
        )
        both = jnp.dot(lhs, occ_in[...].reshape(8 * BLK, OCC), preferred_element_type=jnp.float32)
        own[k] = both[:BLK]
        part[k] = both[BLK:].astype(jnp.bfloat16)
        cp = copy(part.at[k], part_in.at[k], s_part.at[k], r_part.at[k], near(0, 0, 2, 0))
        cp.start()
        started.append(cp)
        facing[k] = cp
    along = []
    for k in ORDER:
        facing[k].wait_recv()
        own[k] += part_in[k].astype(jnp.float32)
        if k:
            mid[k] = own[k].astype(jnp.bfloat16)
            cp = copy(mid.at[k], mid_in.at[k], s_mid.at[k], r_mid.at[k], near(0, 2 * k, 0, 0))
            cp.start()
            started.append(cp)
            along.append((k, cp))
    total = own[0]
    for k, cp in along:
        cp.wait_recv()
        total = total + mid_in[k].astype(jnp.float32)
    fitted = total.astype(jnp.bfloat16)
    rows[0] = fitted
    cols[zp] = fitted

    across = {}
    for r in (1, 2, 3, 6, 7, 4, 5):
        dx, e = ROWS[r]
        cp = copy(rows.at[0], rows.at[r], s_row.at[r], r_row.at[r], near(0, 0, -dx, e))
        cp.start()
        across[r] = cp
        started.append(cp)
    up = []
    for d in (2, 1, 3, 0):
        there = (zp + d) % 4
        if d:
            tz = 2 * there + jnp.where(there < zp, zs, 1 - zs)
            cp = copy(rows.at[0], cols.at[zp], s_col.at[d], r_col.at[d], (y, shell_of(tz)))
        else:
            cp = copy(rows.at[0], cols.at[4], s_col.at[d], r_col.at[d], (y, shell_of(z + 1 - 2 * zs)))
        cp.start()
        started.append(cp)
        up.append(d)
    for d in up:
        there = cols.at[(zp - d + 4) % 4] if d else cols.at[4]
        copy(there, there, s_col.at[d], r_col.at[d], (y, shell_of(z + 1 - 2 * zs))).wait_recv()

    shares = {}
    for q in CHUNKS:
        for r in (2 * q, 2 * q + 1):
            if r:
                across[r].wait_recv()
        block = lax.dot_general(
            rows[2 * q:2 * q + 2].reshape(2 * BLK, OCC), cols[...].reshape(5 * BLK, OCC),
            (((1,), (1,)), ((), ())), preferred_element_type=jnp.float32,
        ).astype(jnp.bfloat16)
        for a in range(5):
            for i in range(2):
                pair[a, 2 * q + i] = block[i * BLK:(i + 1) * BLK, a * BLK:(a + 1) * BLK]
        shares[q] = []
        for dy in (2, 1, 3):
            two = pl.ds(2 * q, 2)
            cp = copy(
                pair.at[(y + dy) % NY, two], pair_in.at[dy, two], s_pair.at[dy, q], r_pair.at[dy, q], near(dy, 0, 0, 0)
            )
            cp.start()
            shares[q].append(cp)
        started += shares[q]
    half = pl.ds(2 * zs, 4)
    to_home = (zp - y + NY) % NY
    twin_send = copy(pair.at[4, half], twin_in.at[to_home], s_twin, r_twin.at[to_home], (zp, shell))

    @pl.when(jnp.logical_not(home))
    def _():
        twin_send.start()

    mirror = {}
    given = {}
    for q in CHUNKS:
        for cp in shares[q]:
            cp.wait_recv()
        two = pl.ds(2 * q, 2)
        value = pair[y, two].astype(jnp.float32)
        for dy in range(1, NY):
            value = value + pair_in[dy, two].astype(jnp.float32)
        done[two] = value.astype(jnp.bfloat16)
        mirror[q] = copy(done.at[two], mirror_in.at[two], s_mirror.at[q], r_mirror.at[q], (zp, shell_of(chosen)))

        @pl.when(jnp.logical_not(home))
        def _(q=q):
            mirror[q].start()

        for r in (2 * q, 2 * q + 1):
            if r:
                dx, e = ROWS[r]
                cp = copy(done.at[r], done_in.at[r], s_done.at[r], r_done.at[r], near(0, 0, dx, e))
                cp.start()
                given[r] = cp
    started += list(given.values())

    def neighbour(i):
        r = 2 * zs + i
        return (y, z * (2 * NX) + ((x + r // 2) % NX) * 2 + (c + r % 2) % 2)

    back = copy(twin_done, twin_mirror, s_back, r_back, (zp, shell_of(z + 1 - 2 * zs)))
    turned = [copy(twin_done.at[i], twin.at[i], s_out.at[i], r_out.at[i], neighbour(i)) for i in range(4)]

    @pl.when(home)
    def _():
        for dy in range(1, NY):
            copy(pair.at[4, half], twin_in.at[dy], s_twin, r_twin.at[dy], (zp, shell)).wait_recv()
        value = pair[4, half].astype(jnp.float32)
        for dy in range(1, NY):
            value = value + twin_in[dy].astype(jnp.float32)
        twin_done[...] = value.astype(jnp.bfloat16)
        back.start()
        for i in range(1, 4):
            turned[i].start()

        @pl.when(zs == 1)
        def _():
            turned[0].start()

    def place(zz, dx, e, value):
        at = ((x + dx + NX) % NX) * 2 + (c + e) % 2
        lane = pl.multiple_of(zz * (8 * BLK) + at * BLK, BLK)
        out_ref[:, pl.ds(lane, BLK)] = value.astype(jnp.float32)

    for q in CHUNKS:
        for r in (2 * q, 2 * q + 1):
            dx, e = ROWS[r]
            if r:
                given[r].wait_recv()
            place(chosen % 2, -dx, e, done_in[r] if r else done[0])

    @pl.when(jnp.logical_not(home))
    def _():
        for q in CHUNKS:
            mirror[q].wait_recv()
            for r in (2 * q, 2 * q + 1):
                dx, e = ROWS[r]
                place(other % 2, dx, e, mirror_in[r].astype(jnp.float32).T)
        twin_send.wait_send()
        for q in CHUNKS:
            mirror[q].wait_send()

    @pl.when(home)
    def _():
        back.wait_recv()
        for i in range(4):
            r = 2 * (1 - zs) + i
            place(1 - zs, r // 2, r % 2, twin_mirror[i].astype(jnp.float32).T)
        for i in range(1, 4):
            turned[i].wait_recv()
            r = 2 * zs + i
            place(1 - zs, -(r // 2), r % 2, twin[i])

        @pl.when(zs == 1)
        def _():
            turned[0].wait_recv()
            place(1 - zs, -1, 0, twin[0])
            turned[0].wait_send()

        @pl.when(zs == 0)
        def _():
            place(1 - zs, 0, 0, twin_done[0])

        back.wait_send()
        for i in range(1, 4):
            turned[i].wait_send()

    for cp in started:
        cp.wait_send()


def body(three_center, occupied, tile_blocks):
    tiles = three_center.reshape(TILES, BLK, BLK)
    targets = tile_blocks.reshape(TILES)
    hit = targets[None, :] == jnp.arange(NZ * NX * 2, dtype=jnp.int32)[:, None]
    slots = jnp.sum(jnp.where(hit, jnp.arange(1, TILES + 1, dtype=jnp.int32)[None, :], 0), axis=1)
    hbm = pl.BlockSpec(memory_space=pltpu.HBM)
    bf16, f32 = jnp.bfloat16, jnp.float32
    dma = pltpu.SemaphoreType.DMA
    return pl.pallas_call(
        kernel,
        out_shape=jax.ShapeDtypeStruct((BLK, 2048), f32),
        in_specs=[pl.BlockSpec(memory_space=pltpu.SMEM), hbm, hbm],
        out_specs=pl.BlockSpec(memory_space=pltpu.VMEM),
        scratch_shapes=[
            pltpu.VMEM((TILES, BLK, BLK), bf16),
            pltpu.VMEM((4, 8, 2, BLK, BLK), bf16),
            pltpu.VMEM((4, 8, 2, BLK, BLK), bf16),
            pltpu.VMEM((8, BLK, OCC), bf16),
            pltpu.VMEM((4, BLK, OCC), f32),
            pltpu.VMEM((4, BLK, OCC), bf16),
            pltpu.VMEM((4, BLK, OCC), bf16),
            pltpu.VMEM((4, BLK, OCC), bf16),
            pltpu.VMEM((4, BLK, OCC), bf16),
            pltpu.VMEM((8, BLK, OCC), bf16),
            pltpu.VMEM((5, BLK, OCC), bf16),
            pltpu.VMEM((5, 8, BLK, BLK), bf16),
            pltpu.VMEM((4, 8, BLK, BLK), bf16),
            pltpu.VMEM((8, BLK, BLK), bf16),
            pltpu.VMEM((8, BLK, BLK), bf16),
            pltpu.VMEM((8, BLK, BLK), bf16),
            pltpu.VMEM((4, 4, BLK, BLK), bf16),
            pltpu.VMEM((4, BLK, BLK), bf16),
            pltpu.VMEM((4, BLK, BLK), bf16),
            pltpu.VMEM((4, BLK, BLK), bf16),
            dma(()), dma(()),
            dma((4, 8)), dma((4, 8)), dma((8,)), dma((8,)), dma((4,)), dma((4,)), dma((4,)), dma((4,)),
            dma((8,)), dma((8,)), dma((4,)), dma((4,)), dma((4, 4)), dma((4, 4)),
            dma((8,)), dma((8,)), dma((4,)), dma((4,)), dma(()), dma((4,)), dma((4,)), dma((4,)), dma(()), dma(()),
        ],
        compiler_params=pltpu.CompilerParams(
            collective_id=0, has_side_effects=True, vmem_limit_bytes=52 * 1024 * 1024
        ),
        cost_estimate=pl.CostEstimate(flops=1_700_000_000, bytes_accessed=3_000_000, transcendentals=0),
    )(slots, tiles, occupied)


def solution(mesh):
    return jax.shard_map(
        body,
        mesh=mesh,
        in_specs=(P("shell", None, "aux", None, None), P("shell", None), P("aux", "shell", None)),
        out_specs=P("shell", "aux"),
        check_vma=False,
    )
```

```python
import jax
import jax.numpy as jnp
from jax import lax
from jax.experimental import pallas as pl
from jax.experimental.pallas import tpu as pltpu
from jax.sharding import PartitionSpec as P

MESH = pl.DeviceIdType.MESH
BLK = 128
OCC = 384
TILES = 40
NY, NZ, NX = 4, 8, 4

WINDOW = [(dz, dx, e) for dz in range(2) for dx in range(2) for e in range(2)]
ROWS = [(dx, e) for dx in range(NX) for e in range(2)]
GROUPS = (((1, 2), (1, 1)), ((1, 3), (1, 0)), ((0, 2), (0, 1)), ((0, 3),), ((0, 0),))
FIRST = (0, 2, 4, 6, 7)
AHEAD = 5
CHUNKS = (0, 1, 2, 3)
RELAYED = (0, 1)
FORWARD = {2: 0, 3: 1}


def greeted():
    out = set()
    for dz, dx, e in WINDOW:
        out.add((0, dz, dx, e))
        out.add((0, -dz % NZ, -dx % NX, e))
    for dz in range(NZ):
        out.add((0, dz, 0, 0))
    for dy in range(NY):
        out.add((dy, 0, 0, 0))
    for dx, e in ROWS:
        out.add((0, 0, dx, e))
    out.discard((0, 0, 0, 0))
    return sorted(out)


def kernel(
    slots_ref, tiles_hbm, occ_hbm, out_ref,
    tiles_ref, dense, tiles_in, occ_in, part, part_in, mid, mid_in, rows, cols, pair, pair_in, done, done_in,
    mirror_in, relay, twin_in, twin, twin_done, twin_mirror,
    s_load, s_load_occ, s_tile, r_tile, s_occ, r_occ, s_part, r_part, s_mid, r_mid, s_row, r_row, s_col, r_col, s_pair, r_pair,
    s_done, r_done, s_mirror, r_mirror, s_relay, r_relay, s_twin, r_twin, s_out, r_out, s_back, r_back,
):
    y = lax.axis_index("aux")
    shell = lax.axis_index("shell")
    z, x, c = shell // (2 * NX), (shell // 2) % NX, shell % 2

    def device(dy, zz, xx, cc):
        return ((y + dy) % NY, zz * (2 * NX) + xx * 2 + cc)

    def near(dy=0, dz=0, dx=0, e=0):
        return device(dy, (z + dz) % NZ, (x + dx) % NX, (c + e) % 2)

    def copy(src, dst, send, recv, to):
        return pltpu.make_async_remote_copy(
            src_ref=src, dst_ref=dst, send_sem=send, recv_sem=recv, device_id=to, device_id_type=MESH
        )

    started = []
    load = pltpu.make_async_copy(tiles_hbm, tiles_ref, s_load)
    load.start()
    load_occ = pltpu.make_async_copy(occ_hbm, occ_in.at[0], s_load_occ)
    load_occ.start()
    peers = greeted()
    barrier = pltpu.get_barrier_semaphore()
    for dy, dz, dx, e in peers:
        pl.semaphore_signal(barrier, inc=1, device_id=near(dy, dz, dx, e), device_id_type=MESH)
    zp, zs = z // 2, z % 2
    home = y == zp
    chosen = jnp.where(home, z, 2 * y + jnp.where(y > zp, zs, 1 - zs))
    other = jnp.where(home, z + 1 - 2 * zs, 2 * y + jnp.where(y > zp, 1 - zs, zs))
    shell_of = lambda zz: zz * (2 * NX) + x * 2 + c
    pl.semaphore_signal(barrier, inc=1, device_id=(zp, shell_of(other)), device_id_type=MESH)

    def target(dz, dx, e):
        tc = (c + e) % 2
        sign = 1 - 2 * tc
        return (z - sign * dz + NZ) % NZ, (x - sign * dx + NX) % NX, tc

    def spread(g):
        for n, (j, k) in enumerate(GROUPS[g]):

            def fill(s, carry, n=FIRST[g] + n, j=j, k=k):
                tz, tx, tc = target(s // 4, (s // 2) % 2, s % 2)
                block = ((tz + 2 * k) % NZ) * (2 * NX) + ((tx + 2 * j) % NX) * 2 + tc
                slot = slots_ref[block]
                held = tiles_ref[jnp.maximum(slot - 1, 0)]
                dense[s, n] = jnp.where(slot > 0, held, jnp.zeros_like(held))
                return carry

            lax.fori_loop(0, 8, fill, 0)

    load_occ.wait()
    pl.semaphore_wait(barrier, len(peers) + 1)
    for s, w in enumerate(WINDOW):
        if s:
            cp = copy(occ_in.at[0], occ_in.at[s], s_occ.at[s], r_occ.at[s], device(0, *target(*w)))
            cp.start()
            started.append(cp)
    orbital = list(started)
    arriving = {}
    load.wait()

    def leave(g):
        here = pl.ds(FIRST[g], len(GROUPS[g]))
        arriving[g] = []
        for s, w in enumerate(WINDOW):
            if s:
                cp = copy(dense.at[s, here], tiles_in.at[s, here], s_tile.at[g, s], r_tile.at[g, s], device(0, *target(*w)))
                cp.start()
                arriving[g].append(cp)

    for g in range(len(GROUPS)):
        spread(g)
        if g < AHEAD:
            leave(g)
    for cp in orbital:
        cp.wait_recv()

    facing = {}
    along = []
    for g, group in enumerate(GROUPS):
        for cp in arriving[g]:
            cp.wait_recv()
        lhs = jnp.concatenate(
            [
                jnp.concatenate([dense[0, n]] + [tiles_in[s, n] for s in range(1, 8)], axis=1)
                for n in range(FIRST[g], FIRST[g] + len(group))
            ],
            axis=0,
        )
        both = jnp.dot(lhs, occ_in[...].reshape(8 * BLK, OCC), preferred_element_type=jnp.float32)
        for n, (j, k) in enumerate(group):
            value = both[n * BLK:(n + 1) * BLK]
            if j:
                part[k] = value.astype(jnp.bfloat16)
                cp = copy(part.at[k], part_in.at[k], s_part.at[k], r_part.at[k], near(0, 0, 2, 0))
                facing[k] = cp
            else:
                facing[k].wait_recv()
                value = value + part_in[k].astype(jnp.float32)
                if k == 0:
                    total = value
                    continue
                mid[k] = value.astype(jnp.bfloat16)
                cp = copy(mid.at[k], mid_in.at[k], s_mid.at[k], r_mid.at[k], near(0, 2 * k, 0, 0))
                along.append((k, cp))
            cp.start()
            started.append(cp)
        for cp in arriving[g]:
            cp.wait_send()
        if g + AHEAD < len(GROUPS):
            leave(g + AHEAD)
    for k, cp in along:
        cp.wait_recv()
        total = total + mid_in[k].astype(jnp.float32)
    fitted = total.astype(jnp.bfloat16)
    rows[0] = fitted
    cols[zp] = fitted

    across = {}
    for r in (1, 2, 3, 4, 5, 6, 7):
        dx, e = ROWS[r]
        cp = copy(rows.at[0], rows.at[r], s_row.at[r], r_row.at[r], near(0, 0, -dx, e))
        cp.start()
        across[r] = cp
        started.append(cp)
    for d in (2, 1, 3, 0):
        there = (zp + d) % 4
        if d:
            tz = 2 * there + jnp.where(there < zp, zs, 1 - zs)
            cp = copy(rows.at[0], cols.at[zp], s_col.at[d], r_col.at[d], (y, shell_of(tz)))
        else:
            cp = copy(rows.at[0], cols.at[4], s_col.at[d], r_col.at[d], (y, shell_of(z + 1 - 2 * zs)))
        cp.start()
        started.append(cp)
    def wait_column(d):
        there = cols.at[(zp - d + 4) % 4] if d else cols.at[4]
        copy(there, there, s_col.at[d], r_col.at[d], (y, shell_of(z + 1 - 2 * zs))).wait_recv()

    def share(dy, q):
        two = pl.ds(2 * q, 2)
        return copy(pair.at[(y + dy) % NY, two], pair_in.at[dy, two], s_pair.at[dy, q], r_pair.at[dy, q], near(dy, 0, 0, 0))

    def product(q, rhs):
        return lax.dot_general(
            rows[2 * q:2 * q + 2].reshape(2 * BLK, OCC), rhs,
            (((1,), (1,)), ((), ())), preferred_element_type=jnp.float32,
        ).astype(jnp.bfloat16)

    def issue(q):
        for r in (2 * q, 2 * q + 1):
            if r:
                across[r].wait_recv()
        if q == 0:
            for d in (0, 1, 3, 2):
                a = (zp - d + 4) % 4
                if d:
                    wait_column(d)
                pair[a, 0:2] = product(q, cols[a]).reshape(2, BLK, BLK)
                dy = (a - y + NY) % NY

                @pl.when(a != y)
                def _(dy=dy):
                    share(dy, 0).start()

            wait_column(0)
            pair[4, 0:2] = product(q, cols[4]).reshape(2, BLK, BLK)
            return
        block = product(q, cols[...].reshape(5 * BLK, OCC))
        for a in range(5):
            for i in range(2):
                pair[a, 2 * q + i] = block[i * BLK:(i + 1) * BLK, a * BLK:(a + 1) * BLK]
        for dy in (2, 1, 3):
            share(dy, q).start()

    half = pl.ds(2 * zs, 4)
    to_home = (zp - y + NY) % NY
    twin_send = copy(pair.at[4, half], twin_in.at[to_home], s_twin, r_twin.at[to_home], (zp, shell))

    mirror = {}
    forward = {}
    given = {}

    def finish(q):
        for dy in (2, 1, 3):
            share(dy, q).wait_recv()
        two = pl.ds(2 * q, 2)
        value = pair[y, two].astype(jnp.float32)
        for dy in range(1, NY):
            value = value + pair_in[dy, two].astype(jnp.float32)
        done[two] = value.astype(jnp.bfloat16)
        mirror[q] = copy(done.at[two], mirror_in.at[two], s_mirror.at[q], r_mirror.at[q], (zp, shell_of(chosen)))
        leaving = mirror[q]
        if q in RELAYED:
            leaving = copy(done.at[two], relay.at[zp, two], s_mirror.at[q], r_relay.at[zp, q], (y, shell_of(chosen)))

        @pl.when(jnp.logical_not(home))
        def _(leaving=leaving):
            leaving.start()

        for r in (2 * q, 2 * q + 1):
            if r:
                dx, e = ROWS[r]
                cp = copy(done.at[r], done_in.at[r], s_done.at[r], r_done.at[r], near(0, 0, dx, e))
                cp.start()
                given[r] = cp
        if q in FORWARD:
            was = FORWARD[q]
            forward[was] = []
            for d in range(1, 4):
                there = (zp + d) % 4
                rest = pl.ds(2 * was, 2)
                forward[was].append(
                    copy(relay.at[there, rest], mirror_in.at[rest], s_relay.at[d, was], r_mirror.at[was], (there, shell))
                )

            @pl.when(home)
            def _(was=was):
                for d, cp in enumerate(forward[was]):
                    there = (zp + d + 1) % 4
                    come = relay.at[there, pl.ds(2 * was, 2)]
                    copy(come, come, s_relay.at[d + 1, was], r_relay.at[there, was], (there, shell)).wait_recv()
                    cp.start()

    for q in range(4):
        issue(q)
        if q == 2:
            @pl.when(jnp.logical_not(home))
            def _():
                twin_send.start()
        if q:
            finish(q - 1)
            for dy in (2, 1, 3):
                share(dy, q - 1).wait_send()
    finish(3)
    for dy in (2, 1, 3):
        share(dy, 3).wait_send()

    started += list(given.values())

    def neighbour(i):
        r = 2 * zs + i
        return (y, z * (2 * NX) + ((x + r // 2) % NX) * 2 + (c + r % 2) % 2)

    back = copy(twin_done, twin_mirror, s_back, r_back, (zp, shell_of(z + 1 - 2 * zs)))
    turned = [copy(twin_done.at[i], twin.at[i], s_out.at[i], r_out.at[i], neighbour(i)) for i in range(4)]

    @pl.when(home)
    def _():
        for dy in range(1, NY):
            copy(pair.at[4, half], twin_in.at[dy], s_twin, r_twin.at[dy], (zp, shell)).wait_recv()
        value = pair[4, half].astype(jnp.float32)
        for dy in range(1, NY):
            value = value + twin_in[dy].astype(jnp.float32)
        twin_done[...] = value.astype(jnp.bfloat16)
        back.start()
        for i in range(1, 4):
            turned[i].start()

        @pl.when(zs == 1)
        def _():
            turned[0].start()

    def place(zz, dx, e, value):
        at = ((x + dx + NX) % NX) * 2 + (c + e) % 2
        lane = pl.multiple_of(zz * (8 * BLK) + at * BLK, BLK)
        out_ref[:, pl.ds(lane, BLK)] = value.astype(jnp.float32)

    for q in CHUNKS:
        for r in (2 * q, 2 * q + 1):
            dx, e = ROWS[r]
            if r:
                given[r].wait_recv()
            place(chosen % 2, -dx, e, done_in[r] if r else done[0])

    @pl.when(jnp.logical_not(home))
    def _():
        for q in CHUNKS:
            mirror[q].wait_recv()
            for r in (2 * q, 2 * q + 1):
                dx, e = ROWS[r]
                place(other % 2, dx, e, mirror_in[r].astype(jnp.float32).T)
        twin_send.wait_send()
        for q in CHUNKS:
            mirror[q].wait_send()

    @pl.when(home)
    def _():
        back.wait_recv()
        for i in range(4):
            r = 2 * (1 - zs) + i
            place(1 - zs, r // 2, r % 2, twin_mirror[i].astype(jnp.float32).T)
        for i in range(1, 4):
            turned[i].wait_recv()
            r = 2 * zs + i
            place(1 - zs, -(r // 2), r % 2, twin[i])

        @pl.when(zs == 1)
        def _():
            turned[0].wait_recv()
            place(1 - zs, -1, 0, twin[0])
            turned[0].wait_send()

        @pl.when(zs == 0)
        def _():
            place(1 - zs, 0, 0, twin_done[0])

        back.wait_send()
        for i in range(1, 4):
            turned[i].wait_send()
        for was in RELAYED:
            for cp in forward[was]:
                cp.wait_send()

    for cp in started:
        cp.wait_send()


def body(three_center, occupied, tile_blocks):
    tiles = three_center.reshape(TILES, BLK, BLK)
    targets = tile_blocks.reshape(TILES)
    hit = targets[None, :] == jnp.arange(NZ * NX * 2, dtype=jnp.int32)[:, None]
    slots = jnp.sum(jnp.where(hit, jnp.arange(1, TILES + 1, dtype=jnp.int32)[None, :], 0), axis=1)
    hbm = pl.BlockSpec(memory_space=pltpu.HBM)
    bf16, f32 = jnp.bfloat16, jnp.float32
    dma = pltpu.SemaphoreType.DMA
    return pl.pallas_call(
        kernel,
        out_shape=jax.ShapeDtypeStruct((BLK, 2048), f32),
        in_specs=[pl.BlockSpec(memory_space=pltpu.SMEM), hbm, hbm],
        out_specs=pl.BlockSpec(memory_space=pltpu.VMEM),
        scratch_shapes=[
            pltpu.VMEM((TILES, BLK, BLK), bf16),
            pltpu.VMEM((8, 8, BLK, BLK), bf16),
            pltpu.VMEM((8, 8, BLK, BLK), bf16),
            pltpu.VMEM((8, BLK, OCC), bf16),
            pltpu.VMEM((4, BLK, OCC), bf16),
            pltpu.VMEM((4, BLK, OCC), bf16),
            pltpu.VMEM((4, BLK, OCC), bf16),
            pltpu.VMEM((4, BLK, OCC), bf16),
            pltpu.VMEM((8, BLK, OCC), bf16),
            pltpu.VMEM((5, BLK, OCC), bf16),
            pltpu.VMEM((5, 8, BLK, BLK), bf16),
            pltpu.VMEM((4, 8, BLK, BLK), bf16),
            pltpu.VMEM((8, BLK, BLK), bf16),
            pltpu.VMEM((8, BLK, BLK), bf16),
            pltpu.VMEM((8, BLK, BLK), bf16),
            pltpu.VMEM((4, 4, BLK, BLK), bf16),
            pltpu.VMEM((4, 4, BLK, BLK), bf16),
            pltpu.VMEM((4, BLK, BLK), bf16),
            pltpu.VMEM((4, BLK, BLK), bf16),
            pltpu.VMEM((4, BLK, BLK), bf16),
            dma(()), dma(()),
            dma((5, 8)), dma((5, 8)), dma((8,)), dma((8,)), dma((4,)), dma((4,)), dma((4,)), dma((4,)),
            dma((8,)), dma((8,)), dma((4,)), dma((4,)), dma((4, 4)), dma((4, 4)),
            dma((8,)), dma((8,)), dma((4,)), dma((4,)), dma((4, 2)), dma((4, 2)), dma(()), dma((4,)), dma((4,)), dma((4,)), dma(()), dma(()),
        ],
        compiler_params=pltpu.CompilerParams(
            collective_id=0, has_side_effects=True, vmem_limit_bytes=52 * 1024 * 1024
        ),
        cost_estimate=pl.CostEstimate(flops=1_700_000_000, bytes_accessed=3_000_000, transcendentals=0),
    )(slots, tiles, occupied)


def solution(mesh):
    return jax.shard_map(
        body,
        mesh=mesh,
        in_specs=(P("shell", None, "aux", None, None), P("shell", None), P("aux", "shell", None)),
        out_specs=P("shell", "aux"),
        check_vma=False,
    )
```

```python
import jax
import jax.numpy as jnp
from jax import lax
from jax.experimental import pallas as pl
from jax.experimental.pallas import tpu as pltpu
from jax.sharding import PartitionSpec as P

MESH = pl.DeviceIdType.MESH
BLK = 128
OCC = 384
TILES = 40
NY, NZ, NX = 4, 8, 4

WINDOW = [(dz, e) for dz in range(2) for e in range(2)]
ROWS = [(dx, e) for dx in range(NX) for e in range(2)]
SERVED = (2, 1, 3, 0)
GROUPS = [((j, k), (i, k)) for k in SERVED for j, i in ((2, 1), (3, 0))]
CHUNKS = (0, 1, 2, 3)
RELAYED = (0, 1)
FORWARD = {2: 0, 3: 1}


def greeted():
    out = set()
    for dz, e in WINDOW:
        out.add((0, dz, 0, e))
        out.add((0, -dz % NZ, 0, e))
    for dz in range(NZ):
        out.add((0, dz, 0, 0))
    for dy in range(NY):
        out.add((dy, 0, 0, 0))
    for dx, e in ROWS:
        out.add((0, 0, dx, e))
    out.discard((0, 0, 0, 0))
    return sorted(out)


def kernel(
    slots_ref, tiles_hbm, occ_hbm, out_ref,
    tiles_ref, dense, tiles_in, occ_in, own, part, part_in, mid, mid_in, rows, cols, pair, pair_in, done, done_in,
    mirror_in, relay, twin_in, twin, twin_done, twin_mirror,
    s_load, s_load_occ, s_tile, r_tile, s_occ, r_occ, s_part, r_part, s_mid, r_mid, s_row, r_row, s_col, r_col, s_pair, r_pair,
    s_done, r_done, s_mirror, r_mirror, s_relay, r_relay, s_twin, r_twin, s_out, r_out, s_back, r_back,
):
    y = lax.axis_index("aux")
    shell = lax.axis_index("shell")
    z, x, c = shell // (2 * NX), (shell // 2) % NX, shell % 2

    def device(dy, zz, xx, cc):
        return ((y + dy) % NY, zz * (2 * NX) + xx * 2 + cc)

    def near(dy=0, dz=0, dx=0, e=0):
        return device(dy, (z + dz) % NZ, (x + dx) % NX, (c + e) % 2)

    def copy(src, dst, send, recv, to):
        return pltpu.make_async_remote_copy(
            src_ref=src, dst_ref=dst, send_sem=send, recv_sem=recv, device_id=to, device_id_type=MESH
        )

    started = []
    load = pltpu.make_async_copy(tiles_hbm, tiles_ref, s_load)
    load.start()
    load_occ = pltpu.make_async_copy(occ_hbm, occ_in.at[0], s_load_occ)
    load_occ.start()
    peers = greeted()
    barrier = pltpu.get_barrier_semaphore()
    for dy, dz, dx, e in peers:
        pl.semaphore_signal(barrier, inc=1, device_id=near(dy, dz, dx, e), device_id_type=MESH)
    zp, zs = z // 2, z % 2
    home = y == zp
    chosen = jnp.where(home, z, 2 * y + jnp.where(y > zp, zs, 1 - zs))
    other = jnp.where(home, z + 1 - 2 * zs, 2 * y + jnp.where(y > zp, 1 - zs, zs))
    shell_of = lambda zz: zz * (2 * NX) + x * 2 + c
    pl.semaphore_signal(barrier, inc=1, device_id=(zp, shell_of(other)), device_id_type=MESH)

    def target(dz, e):
        tc = (c + e) % 2
        sign = 1 - 2 * tc
        return (z - sign * dz + NZ) % NZ, x, tc

    def spread(g):
        for n, (j, k) in enumerate(GROUPS[g]):

            def fill(s, carry, n=2 * g + n, j=j, k=k):
                tz, tx, tc = target(s // 2, s % 2)
                block = ((tz + 2 * k) % NZ) * (2 * NX) + ((tx + j) % NX) * 2 + tc
                slot = slots_ref[block]
                held = tiles_ref[jnp.maximum(slot - 1, 0)]
                dense[s, n] = jnp.where(slot > 0, held, jnp.zeros_like(held))
                return carry

            lax.fori_loop(0, len(WINDOW), fill, 0)

    load_occ.wait()
    pl.semaphore_wait(barrier, len(peers) + 1)
    for s, w in enumerate(WINDOW):
        if s:
            cp = copy(occ_in.at[0], occ_in.at[s], s_occ.at[s], r_occ.at[s], device(0, *target(*w)))
            cp.start()
            started.append(cp)
    orbital = list(started)
    arriving = {}
    load.wait()

    for g in range(len(GROUPS)):
        spread(g)
        here = pl.ds(2 * g, 2)
        arriving[g] = []
        for s, w in enumerate(WINDOW):
            if s:
                cp = copy(dense.at[s, here], tiles_in.at[s, here], s_tile.at[g, s], r_tile.at[g, s], device(0, *target(*w)))
                cp.start()
                arriving[g].append(cp)
        started += arriving[g]
    for cp in orbital:
        cp.wait_recv()

    facing = {}
    along = []

    def add_up(k):
        value = own[k]
        for cp in facing[k]:
            cp.wait_recv()
        for j in range(1, NX):
            value = value + part_in[k * NX + j].astype(jnp.float32)
        if k == 0:
            return value
        mid[k] = value.astype(jnp.bfloat16)
        cp = copy(mid.at[k], mid_in.at[k], s_mid.at[k], r_mid.at[k], near(0, 2 * k, 0, 0))
        cp.start()
        along.append((k, cp))
        started.append(cp)

    for g, group in enumerate(GROUPS):
        for cp in arriving[g]:
            cp.wait_recv()
        lhs = jnp.concatenate(
            [
                jnp.concatenate([dense[0, n]] + [tiles_in[s, n] for s in range(1, len(WINDOW))], axis=1)
                for n in (2 * g, 2 * g + 1)
            ],
            axis=0,
        )
        both = jnp.dot(lhs, occ_in[...].reshape(len(WINDOW) * BLK, OCC), preferred_element_type=jnp.float32)
        for n, (j, k) in enumerate(group):
            value = both[n * BLK:(n + 1) * BLK]
            if j:
                i = k * NX + j
                part[i] = value.astype(jnp.bfloat16)
                cp = copy(part.at[i], part_in.at[i], s_part.at[i], r_part.at[i], near(0, 0, j, 0))
                cp.start()
                facing.setdefault(k, []).append(cp)
                started.append(cp)
            else:
                own[k] = value
    for k in SERVED:
        total = add_up(k)
    for k, cp in along:
        cp.wait_recv()
        total = total + mid_in[k].astype(jnp.float32)
    fitted = total.astype(jnp.bfloat16)
    rows[0] = fitted
    cols[zp] = fitted

    across = {}
    for r in (1, 2, 3, 4, 5, 6, 7):
        dx, e = ROWS[r]
        cp = copy(rows.at[0], rows.at[r], s_row.at[r], r_row.at[r], near(0, 0, -dx, e))
        cp.start()
        across[r] = cp
        started.append(cp)
    for d in (2, 1, 3, 0):
        there = (zp + d) % 4
        if d:
            tz = 2 * there + jnp.where(there < zp, zs, 1 - zs)
            cp = copy(rows.at[0], cols.at[zp], s_col.at[d], r_col.at[d], (y, shell_of(tz)))
        else:
            cp = copy(rows.at[0], cols.at[4], s_col.at[d], r_col.at[d], (y, shell_of(z + 1 - 2 * zs)))
        cp.start()
        started.append(cp)
    def wait_column(d):
        there = cols.at[(zp - d + 4) % 4] if d else cols.at[4]
        copy(there, there, s_col.at[d], r_col.at[d], (y, shell_of(z + 1 - 2 * zs))).wait_recv()

    def share(dy, q):
        two = pl.ds(2 * q, 2)
        return copy(pair.at[(y + dy) % NY, two], pair_in.at[dy, two], s_pair.at[dy, q], r_pair.at[dy, q], near(dy, 0, 0, 0))

    def product(q, rhs):
        return lax.dot_general(
            rows[2 * q:2 * q + 2].reshape(2 * BLK, OCC), rhs,
            (((1,), (1,)), ((), ())), preferred_element_type=jnp.float32,
        ).astype(jnp.bfloat16)

    def issue(q):
        for r in (2 * q, 2 * q + 1):
            if r:
                across[r].wait_recv()
        if q == 0:
            for d in (0, 1, 3, 2):
                a = (zp - d + 4) % 4
                if d:
                    wait_column(d)
                pair[a, 0:2] = product(q, cols[a]).reshape(2, BLK, BLK)
                dy = (a - y + NY) % NY

                @pl.when(a != y)
                def _(dy=dy):
                    share(dy, 0).start()

            wait_column(0)
            pair[4, 0:2] = product(q, cols[4]).reshape(2, BLK, BLK)
            return
        block = product(q, cols[...].reshape(5 * BLK, OCC))
        for a in range(5):
            for i in range(2):
                pair[a, 2 * q + i] = block[i * BLK:(i + 1) * BLK, a * BLK:(a + 1) * BLK]
        for dy in (2, 1, 3):
            share(dy, q).start()

    half = pl.ds(2 * zs, 4)
    to_home = (zp - y + NY) % NY
    twin_send = copy(pair.at[4, half], twin_in.at[to_home], s_twin, r_twin.at[to_home], (zp, shell))

    mirror = {}
    forward = {}
    given = {}

    def finish(q):
        for dy in (2, 1, 3):
            share(dy, q).wait_recv()
        two = pl.ds(2 * q, 2)
        value = pair[y, two].astype(jnp.float32)
        for dy in range(1, NY):
            value = value + pair_in[dy, two].astype(jnp.float32)
        done[two] = value.astype(jnp.bfloat16)
        mirror[q] = copy(done.at[two], mirror_in.at[two], s_mirror.at[q], r_mirror.at[q], (zp, shell_of(chosen)))
        leaving = mirror[q]
        if q in RELAYED:
            leaving = copy(done.at[two], relay.at[zp, two], s_mirror.at[q], r_relay.at[zp, q], (y, shell_of(chosen)))

        @pl.when(jnp.logical_not(home))
        def _(leaving=leaving):
            leaving.start()

        for r in (2 * q, 2 * q + 1):
            if r:
                dx, e = ROWS[r]
                cp = copy(done.at[r], done_in.at[r], s_done.at[r], r_done.at[r], near(0, 0, dx, e))
                cp.start()
                given[r] = cp
        if q in FORWARD:
            was = FORWARD[q]
            forward[was] = []
            for d in range(1, 4):
                there = (zp + d) % 4
                rest = pl.ds(2 * was, 2)
                forward[was].append(
                    copy(relay.at[there, rest], mirror_in.at[rest], s_relay.at[d, was], r_mirror.at[was], (there, shell))
                )

            @pl.when(home)
            def _(was=was):
                for d, cp in enumerate(forward[was]):
                    there = (zp + d + 1) % 4
                    come = relay.at[there, pl.ds(2 * was, 2)]
                    copy(come, come, s_relay.at[d + 1, was], r_relay.at[there, was], (there, shell)).wait_recv()
                    cp.start()

    for q in range(4):
        issue(q)
        if q == 2:
            @pl.when(jnp.logical_not(home))
            def _():
                twin_send.start()
        if q:
            finish(q - 1)
            for dy in (2, 1, 3):
                share(dy, q - 1).wait_send()
    finish(3)
    for dy in (2, 1, 3):
        share(dy, 3).wait_send()

    started += list(given.values())

    def neighbour(i):
        r = 2 * zs + i
        return (y, z * (2 * NX) + ((x + r // 2) % NX) * 2 + (c + r % 2) % 2)

    back = copy(twin_done, twin_mirror, s_back, r_back, (zp, shell_of(z + 1 - 2 * zs)))
    turned = [copy(twin_done.at[i], twin.at[i], s_out.at[i], r_out.at[i], neighbour(i)) for i in range(4)]

    @pl.when(home)
    def _():
        for dy in range(1, NY):
            copy(pair.at[4, half], twin_in.at[dy], s_twin, r_twin.at[dy], (zp, shell)).wait_recv()
        value = pair[4, half].astype(jnp.float32)
        for dy in range(1, NY):
            value = value + twin_in[dy].astype(jnp.float32)
        twin_done[...] = value.astype(jnp.bfloat16)
        back.start()
        for i in range(1, 4):
            turned[i].start()

        @pl.when(zs == 1)
        def _():
            turned[0].start()

    def place(zz, dx, e, value):
        at = ((x + dx + NX) % NX) * 2 + (c + e) % 2
        lane = pl.multiple_of(zz * (8 * BLK) + at * BLK, BLK)
        out_ref[:, pl.ds(lane, BLK)] = value.astype(jnp.float32)

    for q in CHUNKS:
        for r in (2 * q, 2 * q + 1):
            dx, e = ROWS[r]
            if r:
                given[r].wait_recv()
            place(chosen % 2, -dx, e, done_in[r] if r else done[0])

    @pl.when(jnp.logical_not(home))
    def _():
        for q in CHUNKS:
            mirror[q].wait_recv()
            for r in (2 * q, 2 * q + 1):
                dx, e = ROWS[r]
                place(other % 2, dx, e, mirror_in[r].astype(jnp.float32).T)
        twin_send.wait_send()
        for q in CHUNKS:
            mirror[q].wait_send()

    @pl.when(home)
    def _():
        back.wait_recv()
        for i in range(4):
            r = 2 * (1 - zs) + i
            place(1 - zs, r // 2, r % 2, twin_mirror[i].astype(jnp.float32).T)
        for i in range(1, 4):
            turned[i].wait_recv()
            r = 2 * zs + i
            place(1 - zs, -(r // 2), r % 2, twin[i])

        @pl.when(zs == 1)
        def _():
            turned[0].wait_recv()
            place(1 - zs, -1, 0, twin[0])
            turned[0].wait_send()

        @pl.when(zs == 0)
        def _():
            place(1 - zs, 0, 0, twin_done[0])

        back.wait_send()
        for i in range(1, 4):
            turned[i].wait_send()
        for was in RELAYED:
            for cp in forward[was]:
                cp.wait_send()

    for cp in started:
        cp.wait_send()


def body(three_center, occupied, tile_blocks):
    tiles = three_center.reshape(TILES, BLK, BLK)
    targets = tile_blocks.reshape(TILES)
    hit = targets[None, :] == jnp.arange(NZ * NX * 2, dtype=jnp.int32)[:, None]
    slots = jnp.sum(jnp.where(hit, jnp.arange(1, TILES + 1, dtype=jnp.int32)[None, :], 0), axis=1)
    hbm = pl.BlockSpec(memory_space=pltpu.HBM)
    bf16, f32 = jnp.bfloat16, jnp.float32
    dma = pltpu.SemaphoreType.DMA
    return pl.pallas_call(
        kernel,
        out_shape=jax.ShapeDtypeStruct((BLK, 2048), f32),
        in_specs=[pl.BlockSpec(memory_space=pltpu.SMEM), hbm, hbm],
        out_specs=pl.BlockSpec(memory_space=pltpu.VMEM),
        scratch_shapes=[
            pltpu.VMEM((TILES, BLK, BLK), bf16),
            pltpu.VMEM((4, 16, BLK, BLK), bf16),
            pltpu.VMEM((4, 16, BLK, BLK), bf16),
            pltpu.VMEM((4, BLK, OCC), bf16),
            pltpu.VMEM((4, BLK, OCC), f32),
            pltpu.VMEM((16, BLK, OCC), bf16),
            pltpu.VMEM((16, BLK, OCC), bf16),
            pltpu.VMEM((4, BLK, OCC), bf16),
            pltpu.VMEM((4, BLK, OCC), bf16),
            pltpu.VMEM((8, BLK, OCC), bf16),
            pltpu.VMEM((5, BLK, OCC), bf16),
            pltpu.VMEM((5, 8, BLK, BLK), bf16),
            pltpu.VMEM((4, 8, BLK, BLK), bf16),
            pltpu.VMEM((8, BLK, BLK), bf16),
            pltpu.VMEM((8, BLK, BLK), bf16),
            pltpu.VMEM((8, BLK, BLK), bf16),
            pltpu.VMEM((4, 4, BLK, BLK), bf16),
            pltpu.VMEM((4, 4, BLK, BLK), bf16),
            pltpu.VMEM((4, BLK, BLK), bf16),
            pltpu.VMEM((4, BLK, BLK), bf16),
            pltpu.VMEM((4, BLK, BLK), bf16),
            dma(()), dma(()),
            dma((8, 4)), dma((8, 4)), dma((4,)), dma((4,)), dma((16,)), dma((16,)), dma((4,)), dma((4,)),
            dma((8,)), dma((8,)), dma((4,)), dma((4,)), dma((4, 4)), dma((4, 4)),
            dma((8,)), dma((8,)), dma((4,)), dma((4,)), dma((4, 2)), dma((4, 2)), dma(()), dma((4,)), dma((4,)), dma((4,)), dma(()), dma(()),
        ],
        compiler_params=pltpu.CompilerParams(
            collective_id=0, has_side_effects=True, vmem_limit_bytes=52 * 1024 * 1024
        ),
        cost_estimate=pl.CostEstimate(flops=1_700_000_000, bytes_accessed=3_000_000, transcendentals=0),
    )(slots, tiles, occupied)


def solution(mesh):
    return jax.shard_map(
        body,
        mesh=mesh,
        in_specs=(P("shell", None, "aux", None, None), P("shell", None), P("aux", "shell", None)),
        out_specs=P("shell", "aux"),
        check_vma=False,
    )
```

```python
import jax
import jax.numpy as jnp
from jax import lax
from jax.experimental import pallas as pl
from jax.experimental.pallas import tpu as pltpu
from jax.sharding import PartitionSpec as P

MESH = pl.DeviceIdType.MESH
BLK = 128
OCC = 384
TILES = 40
NY, NZ, NX = 4, 8, 4

WINDOW = [(dz, e) for dz in range(2) for e in range(2)]
OFFSET = (0, -2, 3, 1)
AFTER, HERE, BEFORE = 0, 2, 4
ROWS = [(dx, e) for dx in range(NX) for e in range(2)]
SERVED = (2, 3, 1, 0)
GROUPS = (
    ((2, 2), (2, 3)), ((2, 1), (2, 0)), ((3, 2), (3, 3)), ((1, 2), (1, 3)),
    ((1, 1), (3, 1)), ((3, 0), (1, 0)), ((0, 2), (0, 3)), ((0, 1), (0, 0)),
)
CHUNKS = (0, 1, 2, 3)
RELAYED = (0, 1)
FORWARD = {2: 0, 3: 1}


def greeted():
    out = set()
    for dz, e in WINDOW:
        out.add((0, dz, 0, e))
        out.add((0, -dz % NZ, 0, e))
    for dz in range(NZ):
        out.add((0, dz, 0, 0))
    for dy in range(NY):
        out.add((dy, 0, 0, 0))
    for dx, e in ROWS:
        out.add((0, 0, dx, e))
    out.discard((0, 0, 0, 0))
    return sorted(out)


def kernel(
    slots_ref, tiles_hbm, occ_hbm, out_ref,
    tiles_ref, dense, tiles_in, occ_in, own, part, part_in, mid, mid_in, rows, cols, pair, pair_in, done, done_in,
    mirror_in, relay, twin_in, twin, twin_done, twin_mirror,
    s_load, s_load_occ, s_tile, r_tile, s_occ, r_occ, s_part, r_part, s_mid, r_mid, s_row, r_row, s_col, r_col, s_pair, r_pair,
    s_done, r_done, s_mirror, r_mirror, s_relay, r_relay, s_twin, r_twin, s_out, r_out, s_back, r_back,
):
    y = lax.axis_index("aux")
    shell = lax.axis_index("shell")
    z, x, c = shell // (2 * NX), (shell // 2) % NX, shell % 2

    def device(dy, zz, xx, cc):
        return ((y + dy) % NY, zz * (2 * NX) + xx * 2 + cc)

    def near(dy=0, dz=0, dx=0, e=0):
        return device(dy, (z + dz) % NZ, (x + dx) % NX, (c + e) % 2)

    def copy(src, dst, send, recv, to):
        return pltpu.make_async_remote_copy(
            src_ref=src, dst_ref=dst, send_sem=send, recv_sem=recv, device_id=to, device_id_type=MESH
        )

    started = []
    load = pltpu.make_async_copy(tiles_hbm, tiles_ref, s_load)
    load.start()
    load_occ = pltpu.make_async_copy(occ_hbm, occ_in.at[HERE], s_load_occ)
    load_occ.start()
    peers = greeted()
    barrier = pltpu.get_barrier_semaphore()
    for dy, dz, dx, e in peers:
        pl.semaphore_signal(barrier, inc=1, device_id=near(dy, dz, dx, e), device_id_type=MESH)
    zp, zs = z // 2, z % 2
    home = y == zp
    chosen = jnp.where(home, z, 2 * y + jnp.where(y > zp, zs, 1 - zs))
    other = jnp.where(home, z + 1 - 2 * zs, 2 * y + jnp.where(y > zp, 1 - zs, zs))
    shell_of = lambda zz: zz * (2 * NX) + x * 2 + c
    pl.semaphore_signal(barrier, inc=1, device_id=(zp, shell_of(other)), device_id_type=MESH)

    sign = 1 - 2 * c

    def target(dz, e, k):
        tc = (c + e) % 2
        toward = (1 - 2 * tc) * (-1 if k < 2 else 1)
        return (z + toward * dz + NZ) % NZ, x, tc

    def spread(g):
        for n, (j, k) in enumerate(GROUPS[g]):

            def fill(s, carry, n=2 * g + n, j=j, k=k):
                tz, tx, tc = target(s // 2, s % 2, k)
                owner = (tz + (1 - 2 * tc) * OFFSET[k] + NZ) % NZ
                block = owner * (2 * NX) + ((tx + (1 - 2 * tc) * j + NX) % NX) * 2 + tc
                slot = slots_ref[block]
                held = tiles_ref[jnp.maximum(slot - 1, 0)]
                dense[s, n] = jnp.where(slot > 0, held, jnp.zeros_like(held))
                return carry

            lax.fori_loop(0, len(WINDOW), fill, 0)

    load_occ.wait()
    pl.semaphore_wait(barrier, len(peers) + 1)
    def orbit(slot, to_slot, to):
        return copy(occ_in.at[slot], occ_in.at[to_slot], s_occ.at[to_slot], r_occ.at[to_slot], to)

    mate = near(0, 0, 0, 1)
    onward = device(0, (z + sign + NZ) % NZ, x, c)
    backward = device(0, (z - sign + NZ) % NZ, x, c)
    for to_slot, to in ((AFTER, backward), (BEFORE, onward), (HERE + 1, mate)):
        cp = orbit(HERE, to_slot, to)
        cp.start()
        started.append(cp)
    orbital = list(started)
    arriving = {}
    load.wait()

    for g in range(len(GROUPS)):
        spread(g)
        here = pl.ds(2 * g, 2)
        arriving[g] = []
        for s, w in enumerate(WINDOW):
            if s:
                cp = copy(dense.at[s, here], tiles_in.at[s, here], s_tile.at[g, s], r_tile.at[g, s], device(0, *target(*w, GROUPS[g][0][1])))
                cp.start()
                arriving[g].append(cp)
        started += arriving[g]
    for cp, to_slot in zip(orbital, (BEFORE + 1, AFTER + 1)):
        cp.wait_recv()
        cp = orbit(BEFORE + AFTER - to_slot + 1, to_slot, mate)
        cp.start()
        started.append(cp)
        orbital.append(cp)
    for cp in orbital[2:]:
        cp.wait_recv()

    facing = {}
    passing = {}
    along = []

    def add_up(k):
        value = own[k]
        for cp in facing[k]:
            cp.wait_recv()
        for j in (1, 3):
            value = value + part_in[k * NX + j].astype(jnp.float32)
        if k == 0:
            return value
        mid[k] = value.astype(jnp.bfloat16)
        cp = copy(mid.at[k], mid_in.at[k], s_mid.at[k], r_mid.at[k], device(0, (z + sign * OFFSET[k] + NZ) % NZ, x, c))
        cp.start()
        along.append((k, cp))
        started.append(cp)

    for g, group in enumerate(GROUPS):
        for cp in arriving[g]:
            cp.wait_recv()
        lhs = jnp.concatenate(
            [
                jnp.concatenate([dense[0, n]] + [tiles_in[s, n] for s in range(1, len(WINDOW))], axis=1)
                for n in (2 * g, 2 * g + 1)
            ],
            axis=0,
        )
        order = (HERE, HERE + 1, AFTER, AFTER + 1) if group[0][1] < 2 else (HERE, HERE + 1, BEFORE, BEFORE + 1)
        rhs = jnp.concatenate([occ_in[i] for i in order], axis=0)
        both = jnp.dot(lhs, rhs, preferred_element_type=jnp.float32)
        for n, (j, k) in enumerate(group):
            value = both[n * BLK:(n + 1) * BLK]
            if j:
                i = k * NX + j
                if j == 1:
                    passing[k].wait_recv()
                    value = value + part_in[k * NX + 2].astype(jnp.float32)
                part[i] = value.astype(jnp.bfloat16)
                step = -sign if j == 3 else sign
                to = device(0, z, (x + step + NX) % NX, c)
                cp = copy(part.at[i], part_in.at[i], s_part.at[i], r_part.at[i], to)
                cp.start()
                started.append(cp)
                if j == 2:
                    passing[k] = cp
                else:
                    facing.setdefault(k, []).append(cp)
            else:
                own[k] = value
        if g == 6:
            for k in SERVED[:2]:
                add_up(k)
    for k in SERVED[2:]:
        total = add_up(k)
    for k, cp in along:
        cp.wait_recv()
        total = total + mid_in[k].astype(jnp.float32)
    fitted = total.astype(jnp.bfloat16)
    rows[0] = fitted
    cols[zp] = fitted

    across = {}
    for r in (1, 2, 3, 4, 5, 6, 7):
        dx, e = ROWS[r]
        cp = copy(rows.at[0], rows.at[r], s_row.at[r], r_row.at[r], near(0, 0, -dx, e))
        cp.start()
        across[r] = cp
        started.append(cp)
    for d in (2, 1, 3, 0):
        there = (zp + d) % 4
        if d:
            tz = 2 * there + jnp.where(there < zp, zs, 1 - zs)
            cp = copy(rows.at[0], cols.at[zp], s_col.at[d], r_col.at[d], (y, shell_of(tz)))
        else:
            cp = copy(rows.at[0], cols.at[4], s_col.at[d], r_col.at[d], (y, shell_of(z + 1 - 2 * zs)))
        cp.start()
        started.append(cp)
    def wait_column(d):
        there = cols.at[(zp - d + 4) % 4] if d else cols.at[4]
        copy(there, there, s_col.at[d], r_col.at[d], (y, shell_of(z + 1 - 2 * zs))).wait_recv()

    def share(dy, q):
        two = pl.ds(2 * q, 2)
        return copy(pair.at[(y + dy) % NY, two], pair_in.at[dy, two], s_pair.at[dy, q], r_pair.at[dy, q], near(dy, 0, 0, 0))

    def product(q, rhs):
        return lax.dot_general(
            rows[2 * q:2 * q + 2].reshape(2 * BLK, OCC), rhs,
            (((1,), (1,)), ((), ())), preferred_element_type=jnp.float32,
        ).astype(jnp.bfloat16)

    def issue(q):
        for r in (2 * q, 2 * q + 1):
            if r:
                across[r].wait_recv()
        if q == 0:
            for d in (0, 1, 3, 2):
                a = (zp - d + 4) % 4
                if d:
                    wait_column(d)
                pair[a, 0:2] = product(q, cols[a]).reshape(2, BLK, BLK)
                dy = (a - y + NY) % NY

                @pl.when(a != y)
                def _(dy=dy):
                    share(dy, 0).start()

            wait_column(0)
            pair[4, 0:2] = product(q, cols[4]).reshape(2, BLK, BLK)
            return
        block = product(q, cols[...].reshape(5 * BLK, OCC))
        for a in range(5):
            for i in range(2):
                pair[a, 2 * q + i] = block[i * BLK:(i + 1) * BLK, a * BLK:(a + 1) * BLK]
        for dy in (2, 1, 3):
            share(dy, q).start()

    half = pl.ds(2 * zs, 4)
    to_home = (zp - y + NY) % NY
    twin_send = copy(pair.at[4, half], twin_in.at[to_home], s_twin, r_twin.at[to_home], (zp, shell))

    mirror = {}
    forward = {}
    given = {}

    def finish(q):
        for dy in (2, 1, 3):
            share(dy, q).wait_recv()
        two = pl.ds(2 * q, 2)
        value = pair[y, two].astype(jnp.float32)
        for dy in range(1, NY):
            value = value + pair_in[dy, two].astype(jnp.float32)
        done[two] = value.astype(jnp.bfloat16)
        mirror[q] = copy(done.at[two], mirror_in.at[two], s_mirror.at[q], r_mirror.at[q], (zp, shell_of(chosen)))
        leaving = mirror[q]
        if q in RELAYED:
            leaving = copy(done.at[two], relay.at[zp, two], s_mirror.at[q], r_relay.at[zp, q], (y, shell_of(chosen)))

        @pl.when(jnp.logical_not(home))
        def _(leaving=leaving):
            leaving.start()

        for r in (2 * q, 2 * q + 1):
            if r:
                dx, e = ROWS[r]
                cp = copy(done.at[r], done_in.at[r], s_done.at[r], r_done.at[r], near(0, 0, dx, e))
                cp.start()
                given[r] = cp
        if q in FORWARD:
            was = FORWARD[q]
            forward[was] = []
            for d in range(1, 4):
                there = (zp + d) % 4
                rest = pl.ds(2 * was, 2)
                forward[was].append(
                    copy(relay.at[there, rest], mirror_in.at[rest], s_relay.at[d, was], r_mirror.at[was], (there, shell))
                )

            @pl.when(home)
            def _(was=was):
                for d, cp in enumerate(forward[was]):
                    there = (zp + d + 1) % 4
                    come = relay.at[there, pl.ds(2 * was, 2)]
                    copy(come, come, s_relay.at[d + 1, was], r_relay.at[there, was], (there, shell)).wait_recv()
                    cp.start()

    for q in range(4):
        issue(q)
        if q == 2:
            @pl.when(jnp.logical_not(home))
            def _():
                twin_send.start()
        if q:
            finish(q - 1)
            for dy in (2, 1, 3):
                share(dy, q - 1).wait_send()
    finish(3)
    for dy in (2, 1, 3):
        share(dy, 3).wait_send()

    started += list(given.values())

    def neighbour(i):
        r = 2 * zs + i
        return (y, z * (2 * NX) + ((x + r // 2) % NX) * 2 + (c + r % 2) % 2)

    back = copy(twin_done, twin_mirror, s_back, r_back, (zp, shell_of(z + 1 - 2 * zs)))
    turned = [copy(twin_done.at[i], twin.at[i], s_out.at[i], r_out.at[i], neighbour(i)) for i in range(4)]

    @pl.when(home)
    def _():
        for dy in range(1, NY):
            copy(pair.at[4, half], twin_in.at[dy], s_twin, r_twin.at[dy], (zp, shell)).wait_recv()
        value = pair[4, half].astype(jnp.float32)
        for dy in range(1, NY):
            value = value + twin_in[dy].astype(jnp.float32)
        twin_done[...] = value.astype(jnp.bfloat16)
        back.start()
        for i in range(1, 4):
            turned[i].start()

        @pl.when(zs == 1)
        def _():
            turned[0].start()

    def place(zz, dx, e, value):
        at = ((x + dx + NX) % NX) * 2 + (c + e) % 2
        lane = pl.multiple_of(zz * (8 * BLK) + at * BLK, BLK)
        out_ref[:, pl.ds(lane, BLK)] = value.astype(jnp.float32)

    for q in CHUNKS:
        for r in (2 * q, 2 * q + 1):
            dx, e = ROWS[r]
            if r:
                given[r].wait_recv()
            place(chosen % 2, -dx, e, done_in[r] if r else done[0])

    @pl.when(jnp.logical_not(home))
    def _():
        for q in CHUNKS:
            mirror[q].wait_recv()
            for r in (2 * q, 2 * q + 1):
                dx, e = ROWS[r]
                place(other % 2, dx, e, mirror_in[r].astype(jnp.float32).T)
        twin_send.wait_send()
        for q in CHUNKS:
            mirror[q].wait_send()

    @pl.when(home)
    def _():
        back.wait_recv()
        for i in range(4):
            r = 2 * (1 - zs) + i
            place(1 - zs, r // 2, r % 2, twin_mirror[i].astype(jnp.float32).T)
        for i in range(1, 4):
            turned[i].wait_recv()
            r = 2 * zs + i
            place(1 - zs, -(r // 2), r % 2, twin[i])

        @pl.when(zs == 1)
        def _():
            turned[0].wait_recv()
            place(1 - zs, -1, 0, twin[0])
            turned[0].wait_send()

        @pl.when(zs == 0)
        def _():
            place(1 - zs, 0, 0, twin_done[0])

        back.wait_send()
        for i in range(1, 4):
            turned[i].wait_send()
        for was in RELAYED:
            for cp in forward[was]:
                cp.wait_send()

    for cp in started:
        cp.wait_send()


def body(three_center, occupied, tile_blocks):
    tiles = three_center.reshape(TILES, BLK, BLK)
    targets = tile_blocks.reshape(TILES)
    hit = targets[None, :] == jnp.arange(NZ * NX * 2, dtype=jnp.int32)[:, None]
    slots = jnp.sum(jnp.where(hit, jnp.arange(1, TILES + 1, dtype=jnp.int32)[None, :], 0), axis=1)
    hbm = pl.BlockSpec(memory_space=pltpu.HBM)
    bf16, f32 = jnp.bfloat16, jnp.float32
    dma = pltpu.SemaphoreType.DMA
    return pl.pallas_call(
        kernel,
        out_shape=jax.ShapeDtypeStruct((BLK, 2048), f32),
        in_specs=[pl.BlockSpec(memory_space=pltpu.SMEM), hbm, hbm],
        out_specs=pl.BlockSpec(memory_space=pltpu.VMEM),
        scratch_shapes=[
            pltpu.VMEM((TILES, BLK, BLK), bf16),
            pltpu.VMEM((4, 16, BLK, BLK), bf16),
            pltpu.VMEM((4, 16, BLK, BLK), bf16),
            pltpu.VMEM((6, BLK, OCC), bf16),
            pltpu.VMEM((4, BLK, OCC), f32),
            pltpu.VMEM((16, BLK, OCC), bf16),
            pltpu.VMEM((16, BLK, OCC), bf16),
            pltpu.VMEM((4, BLK, OCC), bf16),
            pltpu.VMEM((4, BLK, OCC), bf16),
            pltpu.VMEM((8, BLK, OCC), bf16),
            pltpu.VMEM((5, BLK, OCC), bf16),
            pltpu.VMEM((5, 8, BLK, BLK), bf16),
            pltpu.VMEM((4, 8, BLK, BLK), bf16),
            pltpu.VMEM((8, BLK, BLK), bf16),
            pltpu.VMEM((8, BLK, BLK), bf16),
            pltpu.VMEM((8, BLK, BLK), bf16),
            pltpu.VMEM((4, 4, BLK, BLK), bf16),
            pltpu.VMEM((4, 4, BLK, BLK), bf16),
            pltpu.VMEM((4, BLK, BLK), bf16),
            pltpu.VMEM((4, BLK, BLK), bf16),
            pltpu.VMEM((4, BLK, BLK), bf16),
            dma(()), dma(()),
            dma((8, 4)), dma((8, 4)), dma((6,)), dma((6,)), dma((16,)), dma((16,)), dma((4,)), dma((4,)),
            dma((8,)), dma((8,)), dma((4,)), dma((4,)), dma((4, 4)), dma((4, 4)),
            dma((8,)), dma((8,)), dma((4,)), dma((4,)), dma((4, 2)), dma((4, 2)), dma(()), dma((4,)), dma((4,)), dma((4,)), dma(()), dma(()),
        ],
        compiler_params=pltpu.CompilerParams(
            collective_id=0, has_side_effects=True, vmem_limit_bytes=52 * 1024 * 1024
        ),
        cost_estimate=pl.CostEstimate(flops=1_700_000_000, bytes_accessed=3_000_000, transcendentals=0),
    )(slots, tiles, occupied)


def solution(mesh):
    return jax.shard_map(
        body,
        mesh=mesh,
        in_specs=(P("shell", None, "aux", None, None), P("shell", None), P("aux", "shell", None)),
        out_specs=P("shell", "aux"),
        check_vma=False,
    )
```

```python
import jax
import jax.numpy as jnp
from jax import lax
from jax.experimental import pallas as pl
from jax.experimental.pallas import tpu as pltpu
from jax.sharding import PartitionSpec as P

MESH = pl.DeviceIdType.MESH
BLK = 128
OCC = 384
TILES = 40
NY, NZ, NX = 4, 8, 4

WINDOW = [(dz, e) for dz in range(2) for e in range(2)]
OFFSET = (0, -2, 3, 1)
AFTER, HERE, BEFORE = 0, 2, 4
ROWS = [(dx, e) for dx in range(NX) for e in range(2)]
SERVED = (2, 3, 1, 0)
GROUPS = (
    ((2, 2), (2, 3)), ((2, 1), (2, 0)), ((3, 2), (3, 3)), ((1, 2), (1, 3)),
    ((1, 1), (3, 1)), ((3, 0), (1, 0)), ((0, 2), (0, 3)), ((0, 1), (0, 0)),
)
CHUNKS = (0, 1, 2, 3)
RELAYED = (0, 1)
FORWARD = {2: 0, 3: 1}


def greeted():
    out = set()
    for dz, e in WINDOW:
        out.add((0, dz, 0, e))
        out.add((0, -dz % NZ, 0, e))
    for dz in range(NZ):
        out.add((0, dz, 0, 0))
    for dy in range(NY):
        out.add((dy, 0, 0, 0))
    for dx, e in ROWS:
        out.add((0, 0, dx, e))
    out.discard((0, 0, 0, 0))
    return sorted(out)


def kernel(
    slots_ref, tiles_hbm, occ_hbm, out_ref,
    tiles_ref, dense, tiles_in, occ_in, own, part, part_in, mid, mid_in, rows, cols, pair, pair_in, done, done_in,
    mirror_in, relay, twin_in, twin, twin_done, twin_mirror,
    s_load, s_load_occ, s_tile, r_tile, s_occ, r_occ, s_part, r_part, s_mid, r_mid, s_row, r_row, s_col, r_col, s_pair, r_pair,
    s_done, r_done, s_mirror, r_mirror, s_relay, r_relay, s_twin, r_twin, s_out, r_out, s_back, r_back,
):
    y = lax.axis_index("aux")
    shell = lax.axis_index("shell")
    z, x, c = shell // (2 * NX), (shell // 2) % NX, shell % 2

    def device(dy, zz, xx, cc):
        return ((y + dy) % NY, zz * (2 * NX) + xx * 2 + cc)

    def near(dy=0, dz=0, dx=0, e=0):
        return device(dy, (z + dz) % NZ, (x + dx) % NX, (c + e) % 2)

    def copy(src, dst, send, recv, to):
        return pltpu.make_async_remote_copy(
            src_ref=src, dst_ref=dst, send_sem=send, recv_sem=recv, device_id=to, device_id_type=MESH
        )

    started = []
    load = pltpu.make_async_copy(tiles_hbm, tiles_ref, s_load)
    load.start()
    load_occ = pltpu.make_async_copy(occ_hbm, occ_in.at[HERE], s_load_occ)
    load_occ.start()
    peers = greeted()
    barrier = pltpu.get_barrier_semaphore()
    for dy, dz, dx, e in peers:
        pl.semaphore_signal(barrier, inc=1, device_id=near(dy, dz, dx, e), device_id_type=MESH)
    zp, zs = z // 2, z % 2
    home = y == zp
    chosen = jnp.where(home, z, 2 * y + jnp.where(y > zp, zs, 1 - zs))
    other = jnp.where(home, z + 1 - 2 * zs, 2 * y + jnp.where(y > zp, 1 - zs, zs))
    shell_of = lambda zz: zz * (2 * NX) + x * 2 + c
    pl.semaphore_signal(barrier, inc=1, device_id=(zp, shell_of(other)), device_id_type=MESH)

    sign = 1 - 2 * c

    def target(dz, e, k):
        tc = (c + e) % 2
        toward = (1 - 2 * tc) * (-1 if k < 2 else 1)
        return (z + toward * dz + NZ) % NZ, x, tc

    def spread(g):
        for n, (j, k) in enumerate(GROUPS[g]):

            def fill(s, carry, n=2 * g + n, j=j, k=k):
                tz, tx, tc = target(s // 2, s % 2, k)
                owner = (tz + (1 - 2 * tc) * OFFSET[k] + NZ) % NZ
                block = owner * (2 * NX) + ((tx + (1 - 2 * tc) * j + NX) % NX) * 2 + tc
                slot = slots_ref[block]
                held = tiles_ref[jnp.maximum(slot - 1, 0)]
                dense[s, n] = jnp.where(slot > 0, held, jnp.zeros_like(held))
                return carry

            lax.fori_loop(0, len(WINDOW), fill, 0)

    load_occ.wait()
    pl.semaphore_wait(barrier, len(peers) + 1)
    def orbit(slot, to_slot, to):
        return copy(occ_in.at[slot], occ_in.at[to_slot], s_occ.at[to_slot], r_occ.at[to_slot], to)

    mate = near(0, 0, 0, 1)
    onward = device(0, (z + sign + NZ) % NZ, x, c)
    backward = device(0, (z - sign + NZ) % NZ, x, c)
    for to_slot, to in ((AFTER, backward), (BEFORE, onward), (HERE + 1, mate)):
        cp = orbit(HERE, to_slot, to)
        cp.start()
        started.append(cp)
    orbital = list(started)
    arriving = {}
    load.wait()

    for g in range(len(GROUPS)):
        spread(g)
        here = pl.ds(2 * g, 2)
        arriving[g] = []
        for s, w in enumerate(WINDOW):
            if s:
                cp = copy(dense.at[s, here], tiles_in.at[s, here], s_tile.at[g, s], r_tile.at[g, s], device(0, *target(*w, GROUPS[g][0][1])))
                cp.start()
                arriving[g].append(cp)
        started += arriving[g]
    for cp, to_slot in zip(orbital, (BEFORE + 1, AFTER + 1)):
        cp.wait_recv()
        cp = orbit(BEFORE + AFTER - to_slot + 1, to_slot, mate)
        cp.start()
        started.append(cp)
        orbital.append(cp)
    for cp in orbital[2:]:
        cp.wait_recv()

    facing = {}
    passing = {}
    along = []

    def add_up(k):
        value = own[k]
        for cp in facing[k]:
            cp.wait_recv()
        for j in (1, 3):
            value = value + part_in[k * NX + j].astype(jnp.float32)
        if k == 0:
            return value
        mid[k] = value.astype(jnp.bfloat16)
        cp = copy(mid.at[k], mid_in.at[k], s_mid.at[k], r_mid.at[k], device(0, (z + sign * OFFSET[k] + NZ) % NZ, x, c))
        cp.start()
        along.append((k, cp))
        started.append(cp)

    for g, group in enumerate(GROUPS):
        for cp in arriving[g]:
            cp.wait_recv()
        lhs = jnp.concatenate(
            [
                jnp.concatenate([dense[0, n]] + [tiles_in[s, n] for s in range(1, len(WINDOW))], axis=1)
                for n in (2 * g, 2 * g + 1)
            ],
            axis=0,
        )
        order = (HERE, HERE + 1, AFTER, AFTER + 1) if group[0][1] < 2 else (HERE, HERE + 1, BEFORE, BEFORE + 1)
        rhs = jnp.concatenate([occ_in[i] for i in order], axis=0)
        both = jnp.dot(lhs, rhs, preferred_element_type=jnp.float32)
        for n, (j, k) in enumerate(group):
            value = both[n * BLK:(n + 1) * BLK]
            if j:
                i = k * NX + j
                if j == 1:
                    passing[k].wait_recv()
                    value = value + part_in[k * NX + 2].astype(jnp.float32)
                part[i] = value.astype(jnp.bfloat16)
                step = -sign if j == 3 else sign
                to = device(0, z, (x + step + NX) % NX, c)
                cp = copy(part.at[i], part_in.at[i], s_part.at[i], r_part.at[i], to)
                cp.start()
                started.append(cp)
                if j == 2:
                    passing[k] = cp
                else:
                    facing.setdefault(k, []).append(cp)
            else:
                own[k] = value
        if g == 6:
            for k in SERVED[:2]:
                add_up(k)
    for k in SERVED[2:]:
        total = add_up(k)
    for k, cp in along:
        cp.wait_recv()
        total = total + mid_in[k].astype(jnp.float32)
    fitted = total.astype(jnp.bfloat16)
    rows[0] = fitted
    cols[zp] = fitted

    across = {}
    for r in (1, 2, 3, 4, 5, 6, 7):
        dx, e = ROWS[r]
        cp = copy(rows.at[0], rows.at[r], s_row.at[r], r_row.at[r], near(0, 0, -dx, e))
        cp.start()
        across[r] = cp
        started.append(cp)
    for d in (1, 3, 2, 0):
        there = (zp + d) % 4
        if d:
            tz = 2 * there + jnp.where(there < zp, zs, 1 - zs)
            cp = copy(rows.at[0], cols.at[zp], s_col.at[d], r_col.at[d], (y, shell_of(tz)))
        else:
            cp = copy(rows.at[0], cols.at[4], s_col.at[d], r_col.at[d], (y, shell_of(z + 1 - 2 * zs)))
        cp.start()
        started.append(cp)
    def wait_column(d):
        there = cols.at[(zp - d + 4) % 4] if d else cols.at[4]
        copy(there, there, s_col.at[d], r_col.at[d], (y, shell_of(z + 1 - 2 * zs))).wait_recv()

    def share(dy, q):
        two = pl.ds(2 * q, 2)
        return copy(pair.at[(y + dy) % NY, two], pair_in.at[dy, two], s_pair.at[dy, q], r_pair.at[dy, q], near(dy, 0, 0, 0))

    def product(q, rhs):
        return lax.dot_general(
            rows[2 * q:2 * q + 2].reshape(2 * BLK, OCC), rhs,
            (((1,), (1,)), ((), ())), preferred_element_type=jnp.float32,
        ).astype(jnp.bfloat16)

    def issue(q):
        for r in (2 * q, 2 * q + 1):
            if r:
                across[r].wait_recv()
        if q == 0:
            for d in (0, 1, 3, 2):
                a = (zp - d + 4) % 4
                if d:
                    wait_column(d)
                pair[a, 0:2] = product(q, cols[a]).reshape(2, BLK, BLK)
                dy = (a - y + NY) % NY

                @pl.when(a != y)
                def _(dy=dy):
                    share(dy, 0).start()

            wait_column(0)
            pair[4, 0:2] = product(q, cols[4]).reshape(2, BLK, BLK)
            return
        block = product(q, cols[...].reshape(5 * BLK, OCC))
        for a in range(5):
            for i in range(2):
                pair[a, 2 * q + i] = block[i * BLK:(i + 1) * BLK, a * BLK:(a + 1) * BLK]
        for dy in (1, 3, 2):
            share(dy, q).start()

    half = pl.ds(2 * zs, 4)
    to_home = (zp - y + NY) % NY
    twin_send = copy(pair.at[4, half], twin_in.at[to_home], s_twin, r_twin.at[to_home], (zp, shell))

    mirror = {}
    forward = {}
    given = {}

    def finish(q):
        for dy in (2, 1, 3):
            share(dy, q).wait_recv()
        two = pl.ds(2 * q, 2)
        value = pair[y, two].astype(jnp.float32)
        for dy in range(1, NY):
            value = value + pair_in[dy, two].astype(jnp.float32)
        done[two] = value.astype(jnp.bfloat16)
        mirror[q] = copy(done.at[two], mirror_in.at[two], s_mirror.at[q], r_mirror.at[q], (zp, shell_of(chosen)))
        leaving = mirror[q]
        if q in RELAYED:
            leaving = copy(done.at[two], relay.at[zp, two], s_mirror.at[q], r_relay.at[zp, q], (y, shell_of(chosen)))

        @pl.when(jnp.logical_not(home))
        def _(leaving=leaving):
            leaving.start()

        for r in (2 * q, 2 * q + 1):
            if r:
                dx, e = ROWS[r]
                cp = copy(done.at[r], done_in.at[r], s_done.at[r], r_done.at[r], near(0, 0, dx, e))
                cp.start()
                given[r] = cp
        if q in FORWARD:
            was = FORWARD[q]
            forward[was] = []
            for d in range(1, 4):
                there = (zp + d) % 4
                rest = pl.ds(2 * was, 2)
                forward[was].append(
                    copy(relay.at[there, rest], mirror_in.at[rest], s_relay.at[d, was], r_mirror.at[was], (there, shell))
                )

            @pl.when(home)
            def _(was=was):
                for d, cp in enumerate(forward[was]):
                    there = (zp + d + 1) % 4
                    come = relay.at[there, pl.ds(2 * was, 2)]
                    copy(come, come, s_relay.at[d + 1, was], r_relay.at[there, was], (there, shell)).wait_recv()
                    cp.start()

    for q in range(4):
        issue(q)
        if q == 3:
            while started:
                started.pop().wait_send()
        if q == 2:
            @pl.when(jnp.logical_not(home))
            def _():
                twin_send.start()
        if q:
            finish(q - 1)
            for dy in (2, 1, 3):
                share(dy, q - 1).wait_send()
    finish(3)
    for dy in (2, 1, 3):
        share(dy, 3).wait_send()

    started += list(given.values())

    def neighbour(i):
        r = 2 * zs + i
        return (y, z * (2 * NX) + ((x + r // 2) % NX) * 2 + (c + r % 2) % 2)

    back = copy(twin_done, twin_mirror, s_back, r_back, (zp, shell_of(z + 1 - 2 * zs)))
    turned = [copy(twin_done.at[i], twin.at[i], s_out.at[i], r_out.at[i], neighbour(i)) for i in range(4)]

    @pl.when(home)
    def _():
        for dy in range(1, NY):
            copy(pair.at[4, half], twin_in.at[dy], s_twin, r_twin.at[dy], (zp, shell)).wait_recv()
        value = pair[4, half].astype(jnp.float32)
        for dy in range(1, NY):
            value = value + twin_in[dy].astype(jnp.float32)
        twin_done[...] = value.astype(jnp.bfloat16)
        back.start()
        for i in range(1, 4):
            turned[i].start()

        @pl.when(zs == 1)
        def _():
            turned[0].start()

    def place(zz, dx, e, value):
        at = ((x + dx + NX) % NX) * 2 + (c + e) % 2
        lane = pl.multiple_of(zz * (8 * BLK) + at * BLK, BLK)
        out_ref[:, pl.ds(lane, BLK)] = value.astype(jnp.float32)

    for q in CHUNKS:
        for r in (2 * q, 2 * q + 1):
            dx, e = ROWS[r]
            if r:
                given[r].wait_recv()
            place(chosen % 2, -dx, e, done_in[r] if r else done[0])

    @pl.when(jnp.logical_not(home))
    def _():
        for q in CHUNKS:
            mirror[q].wait_recv()
            for r in (2 * q, 2 * q + 1):
                dx, e = ROWS[r]
                place(other % 2, dx, e, mirror_in[r].astype(jnp.float32).T)
        twin_send.wait_send()
        for q in CHUNKS:
            mirror[q].wait_send()

    @pl.when(home)
    def _():
        back.wait_recv()
        for i in range(4):
            r = 2 * (1 - zs) + i
            place(1 - zs, r // 2, r % 2, twin_mirror[i].astype(jnp.float32).T)
        for i in range(1, 4):
            turned[i].wait_recv()
            r = 2 * zs + i
            place(1 - zs, -(r // 2), r % 2, twin[i])

        @pl.when(zs == 1)
        def _():
            turned[0].wait_recv()
            place(1 - zs, -1, 0, twin[0])
            turned[0].wait_send()

        @pl.when(zs == 0)
        def _():
            place(1 - zs, 0, 0, twin_done[0])

        back.wait_send()
        for i in range(1, 4):
            turned[i].wait_send()
        for was in RELAYED:
            for cp in forward[was]:
                cp.wait_send()

    for cp in started:
        cp.wait_send()


def body(three_center, occupied, tile_blocks):
    tiles = three_center.reshape(TILES, BLK, BLK)
    targets = tile_blocks.reshape(TILES)
    hit = targets[None, :] == jnp.arange(NZ * NX * 2, dtype=jnp.int32)[:, None]
    slots = jnp.sum(jnp.where(hit, jnp.arange(1, TILES + 1, dtype=jnp.int32)[None, :], 0), axis=1)
    hbm = pl.BlockSpec(memory_space=pltpu.HBM)
    bf16, f32 = jnp.bfloat16, jnp.float32
    dma = pltpu.SemaphoreType.DMA
    return pl.pallas_call(
        kernel,
        out_shape=jax.ShapeDtypeStruct((BLK, 2048), f32),
        in_specs=[pl.BlockSpec(memory_space=pltpu.SMEM), hbm, hbm],
        out_specs=pl.BlockSpec(memory_space=pltpu.VMEM),
        scratch_shapes=[
            pltpu.VMEM((TILES, BLK, BLK), bf16),
            pltpu.VMEM((4, 16, BLK, BLK), bf16),
            pltpu.VMEM((4, 16, BLK, BLK), bf16),
            pltpu.VMEM((6, BLK, OCC), bf16),
            pltpu.VMEM((4, BLK, OCC), f32),
            pltpu.VMEM((16, BLK, OCC), bf16),
            pltpu.VMEM((16, BLK, OCC), bf16),
            pltpu.VMEM((4, BLK, OCC), bf16),
            pltpu.VMEM((4, BLK, OCC), bf16),
            pltpu.VMEM((8, BLK, OCC), bf16),
            pltpu.VMEM((5, BLK, OCC), bf16),
            pltpu.VMEM((5, 8, BLK, BLK), bf16),
            pltpu.VMEM((4, 8, BLK, BLK), bf16),
            pltpu.VMEM((8, BLK, BLK), bf16),
            pltpu.VMEM((8, BLK, BLK), bf16),
            pltpu.VMEM((8, BLK, BLK), bf16),
            pltpu.VMEM((4, 4, BLK, BLK), bf16),
            pltpu.VMEM((4, 4, BLK, BLK), bf16),
            pltpu.VMEM((4, BLK, BLK), bf16),
            pltpu.VMEM((4, BLK, BLK), bf16),
            pltpu.VMEM((4, BLK, BLK), bf16),
            dma(()), dma(()),
            dma((8, 4)), dma((8, 4)), dma((6,)), dma((6,)), dma((16,)), dma((16,)), dma((4,)), dma((4,)),
            dma((8,)), dma((8,)), dma((4,)), dma((4,)), dma((4, 4)), dma((4, 4)),
            dma((8,)), dma((8,)), dma((4,)), dma((4,)), dma((4, 2)), dma((4, 2)), dma(()), dma((4,)), dma((4,)), dma((4,)), dma(()), dma(()),
        ],
        compiler_params=pltpu.CompilerParams(
            collective_id=0, has_side_effects=True, vmem_limit_bytes=52 * 1024 * 1024
        ),
        cost_estimate=pl.CostEstimate(flops=1_700_000_000, bytes_accessed=3_000_000, transcendentals=0),
    )(slots, tiles, occupied)


def solution(mesh):
    return jax.shard_map(
        body,
        mesh=mesh,
        in_specs=(P("shell", None, "aux", None, None), P("shell", None), P("aux", "shell", None)),
        out_specs=P("shell", "aux"),
        check_vma=False,
    )
```
